256 devices in a mesh: ctx: 64 (over x, z, core), tp: 4 (over y).
Axes of the slice: x: 4, y: 4, z: 8, core: 2. Of those that a mesh axis runs over, the one named last changes fastest.
Arguments:
- queries: bfloat16 [8192, 4096], P('ctx', 'tp'), may hold values from -6 to 6
- key_vectors: bfloat16 [8192, 4096], P('ctx', 'tp'), may hold values from -6 to 6
- stream_gate: bfloat16 [8192, 4096], P('ctx', 'tp'), may hold values from -15 to 15
- stream_key: bfloat16 [8192, 4096], P('ctx', 'tp'), may hold values from -6 to 6
- stream_value: bfloat16 [8192, 4096], P('ctx', 'tp'), may hold values from -6 to 6
- short_filter: float32 [3, 3, 4096], P(None, None, 'tp'), may hold values from -3 to 3
- long_filter: float32 [4096, 8192], P('tp', 'ctx'), may hold values from -1 to 1
- skip_gain: float32 [4096], P('tp'), may hold values from 0.3 to 1
- out_gain: float32 [4096], P('tp'), may hold values from 0.25 to 1.75
Outputs:
- hyena_out: bfloat16 [8192, 4096], P('ctx', 'tp')
- attn_out: bfloat16 [8192, 4096], P('ctx', 'tp')
The draws below stay inside these ranges and needn't reach their ends.
All inputs are finite; a program needn't handle non-finite values.
Results may differ from the reference program's by a relative error of at most 0.024.
Values may be sent and summed in bfloat16 or wider, within the bound.
A program may use at most 64 MiB of HBM per device.

```python
import math
import jax
import jax.numpy as jnp
from jax import lax

H = 32
DH = 128
HC = 4096
TOKENS = 8192


def draw_queries(key, part):
    key = jax.random.fold_in(key, 3)
    drawn = jnp.clip(jax.random.normal(key, (TOKENS, HC), jnp.float32), -6.0, 6.0)
    return drawn.astype(jnp.bfloat16)


def draw_key_vectors(key, part):
    key = jax.random.fold_in(key, 5)
    drawn = jnp.clip(jax.random.normal(key, (TOKENS, HC), jnp.float32), -6.0, 6.0)
    return drawn.astype(jnp.bfloat16)


def draw_stream_gate(key, part):
    key = jax.random.fold_in(key, 7)
    channel_frac = lax.iota(jnp.float32, HC) / HC
    spread = jnp.exp(jax.random.uniform(jax.random.fold_in(key, 1), (HC,), jnp.float32, 0.0, math.log(10.0)))
    rising = 0.5 + 0.7 * channel_frac
    noise_draw = jnp.clip(jax.random.normal(jax.random.fold_in(key, 2), (TOKENS, HC), jnp.float32), -4.0, 4.0)
    levels = spread * rising * 0.3
    return (noise_draw * levels[None, :]).astype(jnp.bfloat16)


def draw_long_filter(key, part):
    key = jax.random.fold_in(key, 9)
    decay_rates = jnp.exp(jax.random.uniform(jax.random.fold_in(key, 1), (HC,), jnp.float32, math.log(1.0 / (4.0 * TOKENS)), math.log(1.0 / 40.0)))
    positions = lax.iota(jnp.float32, TOKENS)
    envelope = jnp.exp(-decay_rates[:, None] * positions[None, :])
    amplitude = jnp.sqrt(1.0 - jnp.exp(-2.0 * decay_rates))
    roughness = jnp.clip(jax.random.normal(jax.random.fold_in(key, 2), (HC, TOKENS), jnp.float32), -4.0, 4.0)
    return (amplitude[:, None] * envelope * roughness).astype(jnp.float32)


def level_of(own_key, extent, cuts, least, top_value):
    def one(dim, shards_of):
        draws = jax.random.uniform(jax.random.fold_in(jax.random.fold_in(own_key, 6), dim), (shards_of,), jnp.float32, least / len(cuts), top_value / len(cuts))
        return jnp.repeat(jnp.exp(draws), extent[dim] // shards_of).reshape((-1,) + (1,) * (len(extent) - dim - 1))

    level = one(*cuts[0])
    for cut in cuts[1:]:
        level = level * one(*cut)
    return level


def bell_draw(rng, extent, scale, bound, cuts=(), kind=jnp.bfloat16):
    loudness = level_of(rng, extent, cuts, -0.22, 0.18) if cuts else 1.0
    result = jax.random.normal(rng, extent, jnp.float32) * scale * loudness
    return jnp.minimum(jnp.maximum(result, -bound), bound).astype(kind)


def setup_inputs(seed: int = 0) -> dict:
    streams_of = jax.random.split(jax.random.key(seed), 10)
    return {
        "queries": draw_queries(jax.random.fold_in(streams_of[9], 71), 0),
        "key_vectors": draw_key_vectors(jax.random.fold_in(streams_of[9], 71), 0),
        "stream_gate": draw_stream_gate(jax.random.fold_in(streams_of[9], 71), 0),
        "stream_key": bell_draw(streams_of[3], (TOKENS, HC), 1.0, 6.0, ((0, 64), (1, 4))),
        "stream_value": bell_draw(streams_of[4], (TOKENS, HC), 1.0, 6.0, ((0, 64), (1, 4))),
        "short_filter": bell_draw(streams_of[5], (3, 3, HC), 0.6, 3.0, ((2, 4),), jnp.float32),
        "long_filter": draw_long_filter(jax.random.fold_in(streams_of[9], 71), 0),
        "skip_gain": jnp.clip(0.3 + 0.7 * jax.random.uniform(streams_of[7], (HC,), jnp.float32) ** level_of(streams_of[7], (HC,), ((0, 4),), -0.2, 0.2), 0.3, 1.0),
        "out_gain": jnp.clip(1.0 + 0.15 * jax.random.normal(streams_of[8], (HC,), jnp.float32), 0.25, 1.75),
    }


def featurize(stream, tap_weights):
    values = stream.astype(jnp.float32)
    padded = jnp.pad(values, ((2, 0), (0, 0)))
    mixed_sum = tap_weights[0] * padded[2:] + tap_weights[1] * padded[1:-1] + tap_weights[2] * padded[:-2]
    return mixed_sum.astype(jnp.bfloat16)

def head_attention(operands):
    query_head, key_head, value_head = operands
    block_rows = min(1024, TOKENS)
    starts = jnp.arange(TOKENS // block_rows, dtype=jnp.int32) * block_rows
    key_pos = jnp.arange(TOKENS, dtype=jnp.int32)

    def one_block(start_row):
        query_block = lax.dynamic_slice_in_dim(query_head, start_row, block_rows, 0)
        query_pos = start_row + jnp.arange(block_rows, dtype=jnp.int32)
        scores = jnp.dot(query_block, key_head.T, preferred_element_type=jnp.float32) / jnp.sqrt(jnp.float32(DH))
        visible = key_pos[None, :] <= query_pos[:, None]
        masked = jnp.where(visible, scores, -jnp.inf)
        row_max = lax.optimization_barrier(jnp.max(masked, axis=1, keepdims=True))
        exp_terms = jnp.where(visible, jnp.exp(masked - row_max), 0.0)
        row_total = lax.optimization_barrier(jnp.sum(exp_terms, axis=1, keepdims=True))
        weights = exp_terms.astype(jnp.bfloat16)
        attended = jnp.dot(weights, value_head, preferred_element_type=jnp.float32) / row_total
        return attended.astype(jnp.bfloat16)
    return lax.map(one_block, starts).reshape(TOKENS, DH)

def per_head(array):
    return array.reshape(TOKENS, H, DH).transpose(1, 0, 2)

def reference(queries, key_vectors, stream_gate, stream_key, stream_value, short_filter, long_filter, skip_gain, out_gain):
    gate_feat = featurize(stream_gate, short_filter[0])
    key_feat = featurize(stream_key, short_filter[1])
    value_feat = featurize(stream_value, short_filter[2])
    product = (key_feat.astype(jnp.float32) * value_feat.astype(jnp.float32)).astype(jnp.bfloat16)
    prod_f = product.astype(jnp.float32)
    spectrum = jnp.fft.rfft(prod_f, n=2 * TOKENS, axis=0) * jnp.fft.rfft(long_filter.T, n=2 * TOKENS, axis=0)
    convolved = jnp.fft.irfft(spectrum, n=2 * TOKENS, axis=0)[:TOKENS].astype(jnp.float32)
    hyena_out = (gate_feat.astype(jnp.float32) * (convolved + skip_gain * prod_f)).astype(jnp.bfloat16)
    attended = lax.map(head_attention, (per_head(queries), per_head(key_vectors), per_head(hyena_out)))
    attended = attended.transpose(1, 0, 2).reshape(TOKENS, HC)
    values = attended.astype(jnp.float32)
    mean_square = lax.optimization_barrier(jnp.mean(values * values, axis=1, keepdims=True))
    attn_out = (values * lax.rsqrt(mean_square + 1e-05) * out_gain).astype(jnp.bfloat16)
    return (hyena_out, attn_out)
```

```python
import math

import jax
import jax.numpy as jnp
import numpy as np
from jax import lax
from jax.experimental import pallas as pl
from jax.experimental.pallas import tpu as pltpu
from jax.sharding import PartitionSpec as P

DH = 128
HC = 4096
NC = 64
TOK = 128
PIECE = 16
F32 = jnp.float32
BF16 = jnp.bfloat16


def block_of(dev):
    return (dev // 2) % 8 * 8 + dev // 16 * 2 + dev % 2


def slot_of(dev):
    return dev % 2 * 32 + dev // 2


def dft_constants():
    slots = np.arange(NC)
    first = (2 * (slots % 32) + slots // 32).astype(np.float64)
    freq = np.arange(NC) + 0.25
    inner = np.arange(TOK)
    outer = 2 * np.pi * freq[:, None] * first[None, :] / NC
    turn = 2 * np.pi * freq[:, None] * inner[None, :] / (NC * TOK)
    mix = 2 * np.pi * (inner[:, None] * inner[None, :] % TOK) / TOK
    cos, sin = np.cos(mix), np.sin(mix)
    outer_in = np.concatenate([np.cos(outer), np.sin(outer)], axis=0)
    outer_out = np.concatenate([np.cos(outer), np.sin(outer)], axis=0).T / (NC * TOK)
    inner_in = np.block([[cos, sin], [-sin, cos]])
    inner_out = np.block([[cos, -sin], [sin, cos]])
    turns = np.stack([np.cos(turn), np.sin(turn)])
    return (
        jnp.asarray(outer_in, BF16),
        jnp.asarray(turns, F32),
        jnp.asarray(inner_in, BF16),
        jnp.asarray(inner_out, BF16),
        jnp.asarray(outer_out, BF16),
    )


def rows16(index):
    return pl.ds(pl.multiple_of(index * PIECE, PIECE), PIECE)


def remote(src, dst, send_sem, recv_sem, dev):
    return pltpu.make_async_remote_copy(
        src_ref=src,
        dst_ref=dst,
        send_sem=send_sem,
        recv_sem=recv_sem,
        device_id={"ctx": dev},
        device_id_type=pl.DeviceIdType.MESH,
    )


def wait_bytes(ref, sem):
    pltpu.make_async_copy(ref, ref, sem).wait()


def mix_taps(stream, halo, taps, which, cols):
    values = stream[:, cols].astype(F32)
    behind = halo[which, :, cols].astype(F32)
    row = lax.broadcasted_iota(jnp.int32, values.shape, 0)
    once = jnp.where(row == 0, behind[15:16], pltpu.roll(values, 1, 0))
    twice = pltpu.roll(values, 2, 0)
    twice = jnp.where(row == 0, behind[14:15], jnp.where(row == 1, behind[15:16], twice))
    mixed = (
        taps[which, 0:1, cols] * values
        + taps[which, 1:2, cols] * once
        + taps[which, 2:3, cols] * twice
    )
    return mixed.astype(BF16)


def spectrum(recv, wide, half, spec, outer_in, turns, inner_in):
    wide[...] = recv[...].astype(F32)
    turn_re, turn_im = turns[0], turns[1]
    for chan in range(0, PIECE, 2):
        pair = [wide[pl.ds(chan + k, NC, stride=PIECE), :].astype(BF16) for k in range(2)]
        both = jnp.dot(outer_in[...], jnp.concatenate(pair, axis=1), preferred_element_type=F32)
        for k in range(2):
            re, im = both[:NC, k * TOK : (k + 1) * TOK], both[NC:, k * TOK : (k + 1) * TOK]
            at = pl.ds((chan + k) * NC, NC)
            half[at, 0:TOK] = (re * turn_re - im * turn_im).astype(BF16)
            half[at, TOK : 2 * TOK] = (re * turn_im + im * turn_re).astype(BF16)
    for part in range(4):
        at = pl.ds(part * 256, 256)
        spec[at, :] = jnp.dot(half[at, :], inner_in[...], preferred_element_type=F32)


def multiply_back(spec_x, spec_h, half, wide, turns, inner_out, outer_out):
    turn_re, turn_im = turns[0], turns[1]
    for part in range(4):
        at = pl.ds(part * 256, 256)
        xr, xi = spec_x[at, 0:TOK], spec_x[at, TOK : 2 * TOK]
        hr, hi = spec_h[at, 0:TOK], spec_h[at, TOK : 2 * TOK]
        half[at, 0:TOK] = (xr * hr - xi * hi).astype(BF16)
        half[at, TOK : 2 * TOK] = (xr * hi + xi * hr).astype(BF16)
    for chan in range(0, PIECE, 2):
        back = jnp.dot(
            half[pl.ds(chan * NC, 2 * NC), :], inner_out[...], preferred_element_type=F32
        )
        pair = []
        for k in range(2):
            re, im = back[k * NC : (k + 1) * NC, :TOK], back[k * NC : (k + 1) * NC, TOK:]
            turned = jnp.concatenate(
                [re * turn_re + im * turn_im, im * turn_re - re * turn_im], axis=0
            )
            pair.append(turned.astype(BF16))
        both = jnp.dot(outer_out[...], jnp.concatenate(pair, axis=1), preferred_element_type=F32)
        for k in range(2):
            wide[pl.ds(chan + k, NC, stride=PIECE), :] = both[:, k * TOK : (k + 1) * TOK]


def hyena_kernel(
    stream_gate,
    stream_key,
    stream_value,
    taps,
    long_filter,
    skip_gain,
    outer_in,
    turns,
    inner_in,
    inner_out,
    outer_out,
    out,
    halo,
    filt_send,
    prod_send,
    gate_send,
    filt_recv,
    prod_recv,
    gate_recv,
    hyena,
    home,
    wide,
    half,
    spec_x,
    spec_h,
    column,
    send_sem,
    recv_sem,
    halo_send,
    halo_recv,
):
    me = lax.axis_index("ctx")
    my_block, my_slot = block_of(me), slot_of(me)
    barrier = pltpu.get_barrier_semaphore()

    def greet(step, unused):
        pl.semaphore_signal(
            barrier,
            inc=1,
            device_id={"ctx": lax.rem(me + step, NC)},
            device_id_type=pl.DeviceIdType.MESH,
        )
        return unused

    lax.fori_loop(1, NC, greet, 0)
    filt_send[...] = long_filter[...].astype(BF16)

    @pl.when(me == 0)
    def _():
        halo[...] = jnp.zeros_like(halo)

    pl.semaphore_wait(barrier, NC - 1)

    streams = (stream_gate, stream_key, stream_value)

    @pl.when(me < NC - 1)
    def _():
        for which, stream in enumerate(streams):
            remote(
                stream.at[pl.ds(TOK - 16, 16), :],
                halo.at[which],
                halo_send.at[which],
                halo_recv.at[which],
                me + 1,
            ).start()

    def scatter(send, recv, index):
        def one(step, unused):
            dev = lax.rem(me + step, NC)
            remote(
                send.at[rows16(block_of(dev)), :],
                recv.at[rows16(my_slot), :],
                send_sem.at[index],
                recv_sem.at[index],
                dev,
            ).start()
            return unused

        lax.fori_loop(1, NC, one, 0)
        recv[rows16(my_slot), :] = send[rows16(my_block), :]

    rest = pl.ds(0, (NC - 1) * PIECE)
    scatter(filt_send, filt_recv, 0)

    @pl.when(me > 0)
    def _():
        for which in range(3):
            wait_bytes(halo.at[which], halo_recv.at[which])

    def columns(head, unused):
        cols = pl.ds(pl.multiple_of(head * DH, DH), DH)
        key_feat = mix_taps(stream_key, halo, taps, 1, cols)
        value_feat = mix_taps(stream_value, halo, taps, 2, cols)
        product = key_feat.astype(F32) * value_feat.astype(F32)
        prod_send[cols, :] = product.T.astype(BF16)
        return unused

    lax.fori_loop(0, 8, columns, 0)
    scatter(prod_send, prod_recv, 1)

    def gate_columns(head, unused):
        cols = pl.ds(pl.multiple_of(head * DH, DH), DH)
        gate_feat = mix_taps(stream_gate, halo, taps, 0, cols)
        gate_send[cols, :] = gate_feat.astype(F32).T.astype(BF16)
        return unused

    lax.fori_loop(0, 8, gate_columns, 0)
    scatter(gate_send, gate_recv, 2)

    head_row = skip_gain[pl.ds((me // 2) % 8, 1), :]
    column[...] = jnp.broadcast_to(head_row, (DH, DH)).T
    skip_tile = column[rows16(my_block % 8), :]

    wait_bytes(filt_recv.at[rest, :], recv_sem.at[0])
    spectrum(filt_recv, wide, half, spec_h, outer_in, turns, inner_in)
    wait_bytes(prod_recv.at[rest, :], recv_sem.at[1])
    spectrum(prod_recv, wide, half, spec_x, outer_in, turns, inner_in)
    multiply_back(spec_x, spec_h, half, wide, turns, inner_out, outer_out)
    wait_bytes(gate_recv.at[rest, :], recv_sem.at[2])
    skip_rows = jnp.concatenate([skip_tile] * 8, axis=0)

    def gated(part, unused):
        at = pl.ds(pl.multiple_of(part * 128, 128), 128)
        inner = wide[at, :] + skip_rows * prod_recv[at, :].astype(F32)
        hyena[at, :] = (gate_recv[at, :].astype(F32) * inner).astype(BF16)
        return unused

    lax.fori_loop(0, 8, gated, 0)

    def go_home(step, unused):
        dev = lax.rem(me + step, NC)
        remote(
            hyena.at[rows16(slot_of(dev)), :],
            home.at[rows16(my_block), :],
            send_sem.at[3],
            recv_sem.at[3],
            dev,
        ).start()
        return unused

    lax.fori_loop(1, NC, go_home, 0)
    home[rows16(my_block), :] = hyena[rows16(my_slot), :]
    wait_bytes(home.at[rest, :], recv_sem.at[3])

    def finish(head, unused):
        cols = pl.ds(pl.multiple_of(head * DH, DH), DH)
        out[:, cols] = home[cols, :].astype(F32).T.astype(BF16)
        return unused

    lax.fori_loop(0, 8, finish, 0)

    for index, send in enumerate((filt_send, prod_send, gate_send, hyena)):
        wait_bytes(send.at[rest, :], send_sem.at[index])

    @pl.when(me < NC - 1)
    def _():
        for which, stream in enumerate(streams):
            wait_bytes(stream.at[pl.ds(TOK - 16, 16), :], halo_send.at[which])


def hyena(stream_gate, stream_key, stream_value, short_filter, long_filter, skip_gain):
    vmem = pl.BlockSpec(memory_space=pltpu.VMEM)
    flat = pltpu.VMEM((NC * PIECE, TOK), BF16)
    return pl.pallas_call(
        hyena_kernel,
        out_shape=jax.ShapeDtypeStruct(stream_gate.shape, BF16),
        in_specs=[vmem] * 11,
        out_specs=vmem,
        scratch_shapes=[
            pltpu.VMEM((3, 16, 1024), BF16),
            flat, flat, flat, flat, flat, flat, flat, flat,
            pltpu.VMEM((NC * PIECE, TOK), F32),
            pltpu.VMEM((NC * PIECE, 2 * TOK), BF16),
            pltpu.VMEM((NC * PIECE, 2 * TOK), F32),
            pltpu.VMEM((NC * PIECE, 2 * TOK), F32),
            pltpu.VMEM((DH, DH), F32),
            pltpu.SemaphoreType.DMA((4,)),
            pltpu.SemaphoreType.DMA((4,)),
            pltpu.SemaphoreType.DMA((3,)),
            pltpu.SemaphoreType.DMA((3,)),
        ],
        compiler_params=pltpu.CompilerParams(
            collective_id=0, has_side_effects=True, vmem_limit_bytes=40 * 2**20
        ),
    )(
        stream_gate, stream_key, stream_value, short_filter, long_filter,
        skip_gain.reshape(8, DH), *dft_constants(),
    )


def to_groups(array, groups, depth_size):
    tok_rows = array.shape[0]
    heads_here = array.shape[1] // depth_size
    piece_rows = tok_rows // groups
    regrouped = array.reshape(groups, piece_rows, heads_here, depth_size).transpose(2, 0, 1, 3)
    return regrouped.reshape(groups * heads_here, piece_rows, depth_size)


def attend_block(query_block, query_pos, kv_blocks, head_size):
    block_rows = query_block.shape[0]
    key_block = kv_blocks.shape[1]

    def advance(state_carry, operands):
        run_max, run_sum, accumulated = state_carry
        kv_block, key_start = operands
        scores = jnp.einsum(
            "qd,kd->qk", query_block, kv_block[:, :head_size], preferred_element_type=jnp.float32
        ) / jnp.sqrt(jnp.float32(head_size))
        key_pos = key_start + lax.iota(jnp.int32, key_block)
        visible = key_pos[None, :] <= query_pos[:, None]
        block_max = jnp.max(jnp.where(visible, scores, -1e30), axis=1)
        new_max = jnp.maximum(run_max, block_max)
        exp_terms = jnp.where(visible, jnp.exp(scores - new_max[:, None]), 0.0)
        factor = jnp.exp(run_max - new_max)
        run_sum = factor * run_sum + jnp.sum(exp_terms, axis=1)
        accumulated = factor[:, None] * accumulated + jnp.dot(
            exp_terms.astype(jnp.bfloat16),
            kv_block[:, head_size:],
            preferred_element_type=jnp.float32,
        )
        return ((new_max, run_sum, accumulated), None)

    starts = lax.iota(jnp.int32, kv_blocks.shape[0]) * key_block
    initial = (
        jnp.full((block_rows,), -1e30, jnp.float32),
        jnp.zeros((block_rows,), jnp.float32),
        jnp.zeros((block_rows, head_size), jnp.float32),
    )
    (run_max, run_sum, accumulated), unused = lax.scan(advance, initial, (kv_blocks, starts))
    return (accumulated / run_sum[:, None]).astype(jnp.bfloat16)


def shards(
    queries,
    key_vectors,
    stream_gate,
    stream_key,
    stream_value,
    short_filter,
    long_filter,
    skip_gain,
    out_gain,
):
    tok_rows, width_here = stream_gate.shape
    ctx_count = lax.axis_size("ctx")
    length = tok_rows * ctx_count
    hyena_out = hyena(
        stream_gate, stream_key, stream_value, short_filter, long_filter, skip_gain
    )
    head_size = DH
    heads_here = width_here // head_size
    group_size = ctx_count // heads_here
    piece_rows = tok_rows // group_size
    query_all = lax.all_to_all(
        to_groups(queries, group_size, head_size), "ctx", split_axis=0, concat_axis=1, tiled=True
    ).reshape(ctx_count * piece_rows, head_size)
    kv_local = jnp.concatenate(
        [
            key_vectors.reshape(tok_rows, heads_here, head_size),
            hyena_out.reshape(tok_rows, heads_here, head_size),
        ],
        axis=2,
    )
    copies = jnp.repeat(kv_local.transpose(1, 0, 2), group_size, axis=0)
    all_kv = lax.all_to_all(copies, "ctx", split_axis=0, concat_axis=1, tiled=True).reshape(
        length, 2 * head_size
    )
    sub_index = lax.axis_index("ctx") % group_size
    query_total = ctx_count * piece_rows
    row_ids = lax.iota(jnp.int32, query_total)
    query_pos = row_ids // piece_rows * tok_rows + sub_index * piece_rows + row_ids % piece_rows
    query_block = min(512, query_total)
    key_block = min(1024, length)
    pieces_out = []
    for block_index in range(query_total // query_block):
        last_source = ((block_index + 1) * query_block - 1) // piece_rows
        reach_keys = (last_source + 1) * tok_rows
        key_count = -(-reach_keys // key_block)
        kv_blocks = all_kv[: key_count * key_block].reshape(key_count, key_block, 2 * head_size)
        row_start = block_index * query_block
        pieces_out.append(
            attend_block(
                query_all[row_start : row_start + query_block],
                query_pos[row_start : row_start + query_block],
                kv_blocks,
                head_size,
            )
        )
    attended = jnp.concatenate(pieces_out, axis=0).reshape(ctx_count, piece_rows, head_size)
    homed = lax.all_to_all(attended, "ctx", split_axis=0, concat_axis=0, tiled=True)
    homed = (
        homed.reshape(heads_here, group_size, piece_rows, head_size)
        .transpose(1, 2, 0, 3)
        .reshape(tok_rows, width_here)
    )
    values = homed.astype(jnp.float32)
    sums = lax.psum(jnp.sum(values * values, axis=1), "tp")
    inverse = lax.rsqrt(sums / HC + 1e-05)
    attn_out = (values * inverse[:, None] * out_gain).astype(jnp.bfloat16)
    return (hyena_out, attn_out)


def solution(mesh):
    in_specs = (
        P("ctx", "tp"),
        P("ctx", "tp"),
        P("ctx", "tp"),
        P("ctx", "tp"),
        P("ctx", "tp"),
        P(None, None, "tp"),
        P("tp", "ctx"),
        P("tp"),
        P("tp"),
    )
    out_specs = (P("ctx", "tp"), P("ctx", "tp"))
    return jax.shard_map(shards, mesh=mesh, in_specs=in_specs, out_specs=out_specs, check_vma=False)
```

```python
import math

import jax
import jax.numpy as jnp
import numpy as np
from jax import lax
from jax.experimental import pallas as pl
from jax.experimental.pallas import tpu as pltpu
from jax.sharding import PartitionSpec as P

DH = 128
HC = 4096
NC = 64
TOK = 128
PIECE = 16
F32 = jnp.float32
BF16 = jnp.bfloat16
SPAN = 512
QB = 256
LOW = -1e30
SCALE = math.log2(math.e) / math.sqrt(DH)


def block_of(dev):
    return (dev // 2) % 8 * 8 + dev // 16 * 2 + dev % 2


def slot_of(dev):
    return dev % 2 * 32 + dev // 2


def dft_constants():
    slots = np.arange(NC)
    first = (2 * (slots % 32) + slots // 32).astype(np.float64)
    freq = np.arange(NC) + 0.25
    inner = np.arange(TOK)
    outer = 2 * np.pi * freq[:, None] * first[None, :] / NC
    turn = 2 * np.pi * freq[:, None] * inner[None, :] / (NC * TOK)
    mix = 2 * np.pi * (inner[:, None] * inner[None, :] % TOK) / TOK
    cos, sin = np.cos(mix), np.sin(mix)
    outer_in = np.concatenate([np.cos(outer), np.sin(outer)], axis=0)
    outer_out = np.concatenate([np.cos(outer), np.sin(outer)], axis=0).T / (NC * TOK)
    inner_in = np.block([[cos, sin], [-sin, cos]])
    inner_out = np.block([[cos, -sin], [sin, cos]])
    turns = np.stack([np.cos(turn), np.sin(turn)])
    return (
        jnp.asarray(outer_in, BF16),
        jnp.asarray(turns, F32),
        jnp.asarray(inner_in, BF16),
        jnp.asarray(inner_out, BF16),
        jnp.asarray(outer_out, BF16),
    )


def rows16(index):
    return pl.ds(pl.multiple_of(index * PIECE, PIECE), PIECE)


def remote(src, dst, send_sem, recv_sem, dev):
    return pltpu.make_async_remote_copy(
        src_ref=src,
        dst_ref=dst,
        send_sem=send_sem,
        recv_sem=recv_sem,
        device_id={"ctx": dev},
        device_id_type=pl.DeviceIdType.MESH,
    )


def remote_tp(src, dst, send_sem, recv_sem, dev):
    return pltpu.make_async_remote_copy(
        src_ref=src,
        dst_ref=dst,
        send_sem=send_sem,
        recv_sem=recv_sem,
        device_id={"tp": dev},
        device_id_type=pl.DeviceIdType.MESH,
    )


def wait_bytes(ref, sem):
    pltpu.make_async_copy(ref, ref, sem).wait()


def mix_taps(stream, halo, taps, which, cols):
    values = stream[:, cols].astype(F32)
    behind = halo[which, :, cols].astype(F32)
    row = lax.broadcasted_iota(jnp.int32, values.shape, 0)
    once = jnp.where(row == 0, behind[15:16], pltpu.roll(values, 1, 0))
    twice = pltpu.roll(values, 2, 0)
    twice = jnp.where(row == 0, behind[14:15], jnp.where(row == 1, behind[15:16], twice))
    mixed = (
        taps[which, 0:1, cols] * values
        + taps[which, 1:2, cols] * once
        + taps[which, 2:3, cols] * twice
    )
    return mixed.astype(BF16)


def spectrum(recv, wide, half, spec, outer_in, turns, inner_in):
    wide[...] = recv[...].astype(F32)
    turn_re, turn_im = turns[0], turns[1]
    for chan in range(0, PIECE, 2):
        pair = [wide[pl.ds(chan + k, NC, stride=PIECE), :].astype(BF16) for k in range(2)]
        both = jnp.dot(outer_in[...], jnp.concatenate(pair, axis=1), preferred_element_type=F32)
        for k in range(2):
            re, im = both[:NC, k * TOK : (k + 1) * TOK], both[NC:, k * TOK : (k + 1) * TOK]
            at = pl.ds((chan + k) * NC, NC)
            half[at, 0:TOK] = (re * turn_re - im * turn_im).astype(BF16)
            half[at, TOK : 2 * TOK] = (re * turn_im + im * turn_re).astype(BF16)
    for part in range(4):
        at = pl.ds(part * 256, 256)
        spec[at, :] = jnp.dot(half[at, :], inner_in[...], preferred_element_type=F32)


def multiply_back(spec_x, spec_h, half, wide, turns, inner_out, outer_out):
    turn_re, turn_im = turns[0], turns[1]
    for part in range(4):
        at = pl.ds(part * 256, 256)
        xr, xi = spec_x[at, 0:TOK], spec_x[at, TOK : 2 * TOK]
        hr, hi = spec_h[at, 0:TOK], spec_h[at, TOK : 2 * TOK]
        half[at, 0:TOK] = (xr * hr - xi * hi).astype(BF16)
        half[at, TOK : 2 * TOK] = (xr * hi + xi * hr).astype(BF16)
    for chan in range(0, PIECE, 2):
        back = jnp.dot(
            half[pl.ds(chan * NC, 2 * NC), :], inner_out[...], preferred_element_type=F32
        )
        pair = []
        for k in range(2):
            re, im = back[k * NC : (k + 1) * NC, :TOK], back[k * NC : (k + 1) * NC, TOK:]
            turned = jnp.concatenate(
                [re * turn_re + im * turn_im, im * turn_re - re * turn_im], axis=0
            )
            pair.append(turned.astype(BF16))
        both = jnp.dot(outer_out[...], jnp.concatenate(pair, axis=1), preferred_element_type=F32)
        for k in range(2):
            wide[pl.ds(chan + k, NC, stride=PIECE), :] = both[:, k * TOK : (k + 1) * TOK]


def attend_scores(
    block, core, across, queries, keys, scores, weights, stats
):
    own = queries[pl.ds(pl.multiple_of(core * 1024 + block * 128, 128), 128), :]
    other = queries[pl.ds(pl.multiple_of((1 - core) * 1024 + block * 128, 128), 128), :]
    both = jnp.concatenate([own, other], axis=0)

    def chunk_rows(chunk):
        return pl.ds(pl.multiple_of(chunk * SPAN, SPAN), SPAN)

    def chunk_scores(chunk):
        return lax.dot_general(
            keys[chunk_rows(chunk), :],
            both,
            (((1,), (1,)), ((), ())),
            preferred_element_type=F32,
        )

    def first(chunk, run_max):
        here = chunk_scores(chunk)
        scores[chunk_rows(chunk), :] = here
        return jnp.maximum(run_max, here.reshape(SPAN // 8, 8, QB).max(axis=0))

    run_max = lax.fori_loop(0, block, first, jnp.full((8, QB), LOW, F32))
    row = lax.broadcasted_iota(jnp.int32, (SPAN, QB), 0)
    lane = lax.broadcasted_iota(jnp.int32, (SPAN, QB), 1)
    key_pos = row // 128 * 256 + core * 128 + row % 128
    parity = jnp.where(lane < 128, core, 1 - core)
    query_pos = lane % 128 // 32 * 256 + parity * 128 + across * 32 + lane % 32
    here = jnp.where(key_pos <= query_pos, chunk_scores(block), LOW)
    scores[chunk_rows(block), :] = here
    run_max = jnp.maximum(run_max, here.reshape(SPAN // 8, 8, QB).max(axis=0))
    top = run_max.max(axis=0, keepdims=True) * SCALE
    base = block * (block + 1) // 2

    def second(chunk, total):
        terms = jnp.exp2(scores[chunk_rows(chunk), :] * SCALE - top)
        weights[chunk_rows(base + chunk), :] = terms.astype(BF16)
        return total + terms.reshape(SPAN // 8, 8, QB).sum(axis=0)

    total = lax.fori_loop(0, block + 1, second, jnp.zeros((8, QB), F32))
    stats[pl.ds(block, 1), :] = top
    stats[pl.ds(8 + block, 1), :] = total.sum(axis=0, keepdims=True)


def attend_values(block, values, weights, stats, other_stats):
    base = block * (block + 1) // 2

    def one(chunk, total):
        lanes = pl.ds(pl.multiple_of(chunk * SPAN, SPAN), SPAN)
        rows = pl.ds(pl.multiple_of((base + chunk) * SPAN, SPAN), SPAN)
        return total + jnp.dot(
            values[:, lanes], weights[rows, :], preferred_element_type=F32
        )

    total = lax.fori_loop(0, block + 1, one, jnp.zeros((DH, QB), F32))
    top, count = stats[pl.ds(block, 1), :], stats[pl.ds(8 + block, 1), :]
    swap = lambda v: jnp.concatenate([v[:, 128:], v[:, :128]], axis=1)
    other_top = swap(other_stats[pl.ds(block, 1), :])
    other_count = swap(other_stats[pl.ds(8 + block, 1), :])
    both_top = jnp.maximum(top, other_top)
    mine = jnp.exp2(top - both_top)
    whole = mine * count + jnp.exp2(other_top - both_top) * other_count
    return total * (mine / whole)


def kernel(
    queries, key_vectors, stream_gate, stream_key, stream_value,
    taps, long_filter, skip_gain, out_gain,
    outer_in, turns, inner_in, inner_out, outer_out,
    hyena_out, attn_out,
    halo, filt_send, prod_send, gate_send, filt_recv, prod_recv, gate_recv,
    hyena, home, wide, half, spec_x, spec_h, column,
    query_all, key_all, value_all, scores, weights, stats, other_stats,
    own_part, part_send, part_recv, att_send, att_home, squares,
    send_sem, recv_sem, halo_send, halo_recv, part_out, part_in,
):
    me = lax.axis_index("ctx")
    tp = lax.axis_index("tp")
    across, depth, core = me // 16, (me // 2) % 8, me % 2
    pair, sibling = me // 2, me + 1 - 2 * core
    member = across * 2 + core
    my_block, my_slot = block_of(me), slot_of(me)
    barrier = pltpu.get_barrier_semaphore()

    def greet(step, unused):
        pl.semaphore_signal(
            barrier,
            inc=1,
            device_id={"ctx": lax.rem(me + step, NC)},
            device_id_type=pl.DeviceIdType.MESH,
        )
        return unused

    lax.fori_loop(1, NC, greet, 0)
    for step in range(1, 4):
        pl.semaphore_signal(
            barrier,
            inc=1,
            device_id={"tp": lax.rem(tp + step, 4)},
            device_id_type=pl.DeviceIdType.MESH,
        )
    filt_send[...] = long_filter[...].astype(BF16)

    @pl.when(me == 0)
    def _():
        halo[...] = jnp.zeros_like(halo)

    pl.semaphore_wait(barrier, NC - 1 + 3)

    streams = (stream_gate, stream_key, stream_value)

    @pl.when(me < NC - 1)
    def _():
        for which, stream in enumerate(streams):
            remote(
                stream.at[pl.ds(TOK - 16, 16), :],
                halo.at[which],
                halo_send.at[which],
                halo_recv.at[which],
                me + 1,
            ).start()

    def scatter(send, recv, index):
        def one(step, unused):
            dev = lax.rem(me + step, NC)
            remote(
                send.at[rows16(block_of(dev)), :],
                recv.at[rows16(my_slot), :],
                send_sem.at[index],
                recv_sem.at[index],
                dev,
            ).start()
            return unused

        lax.fori_loop(1, NC, one, 0)
        recv[rows16(my_slot), :] = send[rows16(my_block), :]

    rest = pl.ds(0, (NC - 1) * PIECE)
    scatter(filt_send, filt_recv, 0)

    @pl.when(me > 0)
    def _():
        for which in range(3):
            wait_bytes(halo.at[which], halo_recv.at[which])

    def columns(head, unused):
        cols = pl.ds(pl.multiple_of(head * DH, DH), DH)
        key_feat = mix_taps(stream_key, halo, taps, 1, cols)
        value_feat = mix_taps(stream_value, halo, taps, 2, cols)
        product = key_feat.astype(F32) * value_feat.astype(F32)
        prod_send[cols, :] = product.T.astype(BF16)
        return unused

    lax.fori_loop(0, 8, columns, 0)
    scatter(prod_send, prod_recv, 1)

    key_rows = pl.ds(pl.multiple_of(pair * 128, 128), 128)

    def key_out(step, unused):
        head = lax.rem(depth + step, 8)
        remote(
            key_vectors.at[:, pl.ds(pl.multiple_of(head * DH, DH), DH)],
            key_all.at[key_rows, :],
            send_sem.at[4],
            recv_sem.at[4],
            across * 16 + head * 2 + core,
        ).start()
        return unused

    lax.fori_loop(1, 8, key_out, 0)
    my_cols = pl.ds(pl.multiple_of(depth * DH, DH), DH)
    key_all[key_rows, :] = key_vectors[:, my_cols]

    query_rows = pl.ds(pl.multiple_of(core * 1024 + pair * 32, 32), 32)

    def query_out(step, unused):
        goal = lax.rem(pair + step, 32)
        remote(
            queries.at[
                pl.ds(pl.multiple_of(goal // 8 * 32, 32), 32),
                pl.ds(pl.multiple_of(goal % 8 * DH, DH), DH),
            ],
            query_all.at[query_rows, :],
            send_sem.at[5],
            recv_sem.at[5],
            goal * 2 + core,
        ).start()
        return unused

    lax.fori_loop(1, 32, query_out, 0)
    across_rows = pl.ds(pl.multiple_of(across * 32, 32), 32)
    query_all[query_rows, :] = queries[across_rows, my_cols]

    def gate_columns(head, unused):
        cols = pl.ds(pl.multiple_of(head * DH, DH), DH)
        gate_feat = mix_taps(stream_gate, halo, taps, 0, cols)
        gate_send[cols, :] = gate_feat.astype(F32).T.astype(BF16)
        return unused

    lax.fori_loop(0, 8, gate_columns, 0)
    scatter(gate_send, gate_recv, 2)

    head_row = skip_gain[pl.ds(depth, 1), :]
    column[...] = jnp.broadcast_to(head_row, (DH, DH)).T
    skip_tile = column[rows16(my_block % 8), :]

    wait_bytes(filt_recv.at[rest, :], recv_sem.at[0])
    spectrum(filt_recv, wide, half, spec_h, outer_in, turns, inner_in)
    wait_bytes(prod_recv.at[rest, :], recv_sem.at[1])

    wait_bytes(key_all.at[pl.ds(0, 7 * 128), :], recv_sem.at[4])
    keys_here = pl.ds(pl.multiple_of(across * 1024, 1024), 1024)

    def key_on(step, unused):
        remote(
            key_all.at[keys_here, :],
            key_all.at[keys_here, :],
            send_sem.at[6],
            recv_sem.at[6],
            lax.rem(across + step, 4) * 16 + depth * 2 + core,
        ).start()
        return unused

    lax.fori_loop(1, 4, key_on, 0)
    wait_bytes(query_all.at[pl.ds(0, 31 * 32), :], recv_sem.at[5])
    queries_here = pl.ds(pl.multiple_of(core * 1024, 1024), 1024)
    query_on = remote(
        query_all.at[queries_here, :],
        query_all.at[queries_here, :],
        send_sem.at[7],
        recv_sem.at[7],
        sibling,
    )
    query_on.start()

    spectrum(prod_recv, wide, half, spec_x, outer_in, turns, inner_in)
    multiply_back(spec_x, spec_h, half, wide, turns, inner_out, outer_out)
    wait_bytes(gate_recv.at[rest, :], recv_sem.at[2])

    def gated(slot, unused):
        at = rows16(slot)
        inner = wide[at, :] + skip_tile * prod_recv[at, :].astype(F32)
        lanes = pl.ds(pl.multiple_of(slot * TOK, TOK), TOK)
        hyena[:, lanes] = (gate_recv[at, :].astype(F32) * inner).astype(BF16)
        return unused

    lax.fori_loop(0, NC, gated, 0)

    def value_out(step, unused):
        goal = lax.rem(member + step, 8)
        remote(
            hyena.at[:, pl.ds(pl.multiple_of(goal % 2 * 4096, 4096), 4096)],
            value_all.at[rows16(member), :],
            send_sem.at[8],
            recv_sem.at[8],
            goal // 2 * 16 + depth * 2 + goal % 2,
        ).start()
        return unused

    lax.fori_loop(1, 8, value_out, 0)
    value_all[rows16(member), :] = hyena[:, pl.ds(pl.multiple_of(core * 4096, 4096), 4096)]

    def go_home(step, unused):
        dev = lax.rem(me + step, NC)
        remote(
            hyena.at[:, pl.ds(pl.multiple_of(slot_of(dev) * TOK, TOK), TOK)],
            home.at[rows16(my_block), :],
            send_sem.at[3],
            recv_sem.at[3],
            dev,
        ).start()
        return unused

    lax.fori_loop(1, NC, go_home, 0)
    home[rows16(my_block), :] = hyena[:, pl.ds(pl.multiple_of(my_slot * TOK, TOK), TOK)]

    wait_bytes(key_all.at[pl.ds(0, 3 * 1024), :], recv_sem.at[6])
    query_on.wait_recv()

    def scoring(step, unused):
        block = lax.rem(depth + step, 8)
        attend_scores(
            block, core, across, query_all, key_all, scores, weights, stats
        )
        return unused

    lax.fori_loop(0, 8, scoring, 0)
    stats_out = remote(stats, other_stats, send_sem.at[9], recv_sem.at[9], sibling)
    stats_out.start()

    wait_bytes(home.at[rest, :], recv_sem.at[3])

    def finish(head, unused):
        cols = pl.ds(pl.multiple_of(head * DH, DH), DH)
        hyena_out[:, cols] = home[cols, :].astype(F32).T.astype(BF16)
        return unused

    lax.fori_loop(0, 8, finish, 0)

    stats_out.wait_recv()
    wait_bytes(value_all.at[pl.ds(0, 7 * PIECE), :], recv_sem.at[8])

    def part_copy(block):
        return remote(
            part_send.at[block],
            part_recv.at[block],
            part_out.at[block],
            part_in.at[block],
            sibling,
        )

    def settle(block):
        part_copy(block).wait_recv()
        whole = own_part[block] + part_recv[block].astype(F32)
        att_send[pl.ds(pl.multiple_of(block * 128, 128), 128), :] = whole.T.astype(BF16)

        for k in range(4):
            goal = block * 4 + k
            rows = pl.ds(pl.multiple_of(goal * 32, 32), 32)

            @pl.when(goal != pair)
            def _():
                remote(
                    att_send.at[rows, :],
                    att_home.at[across_rows, my_cols],
                    send_sem.at[10],
                    recv_sem.at[10],
                    goal * 2 + core,
                ).start()

            @pl.when(goal == pair)
            def _():
                att_home[across_rows, my_cols] = att_send[rows, :]

    def valuing(step, unused):
        block = lax.rem(depth + step, 8)
        total = attend_values(block, value_all, weights, stats, other_stats)
        own_part[block] = total[:, :128]
        part_send[block] = total[:, 128:].astype(BF16)
        part_copy(block).start()

        @pl.when(step > 0)
        def _():
            settle(lax.rem(depth + step + 7, 8))

        return unused

    lax.fori_loop(0, 8, valuing, 0)
    settle(lax.rem(depth + 7, 8))

    wait_bytes(att_send.at[pl.ds(0, 31 * 32), :], recv_sem.at[10])
    summed = jnp.zeros((TOK, DH), F32)
    for head in range(8):
        part = att_home[:, head * DH : (head + 1) * DH].astype(F32)
        summed = summed + part * part
    squares[tp] = jnp.broadcast_to(summed.T.sum(axis=0, keepdims=True), (8, TOK))
    for step in range(1, 4):
        remote_tp(
            squares.at[tp],
            squares.at[tp],
            send_sem.at[11],
            recv_sem.at[11],
            lax.rem(tp + step, 4),
        ).start()
    wait_bytes(squares.at[pl.ds(0, 3)], recv_sem.at[11])
    mean = (squares[0] + squares[1] + squares[2] + squares[3]) * (1.0 / HC)
    inverse = jnp.broadcast_to(lax.rsqrt(mean + 1e-05)[0:1, :], (TOK, TOK)).T
    for head in range(8):
        cols = slice(head * DH, (head + 1) * DH)
        part = att_home[:, cols].astype(F32)
        attn_out[:, cols] = (part * inverse * out_gain[0:1, cols]).astype(BF16)

    for index, send in enumerate((filt_send, prod_send, gate_send, home)):
        wait_bytes(send.at[rest, :], send_sem.at[index])
    wait_bytes(key_all.at[pl.ds(0, 7 * 128), :], send_sem.at[4])
    wait_bytes(query_all.at[pl.ds(0, 31 * 32), :], send_sem.at[5])
    wait_bytes(key_all.at[pl.ds(0, 3 * 1024), :], send_sem.at[6])
    query_on.wait_send()
    wait_bytes(value_all.at[pl.ds(0, 7 * PIECE), :], send_sem.at[8])
    stats_out.wait_send()
    for block in range(8):
        part_copy(block).wait_send()
    wait_bytes(att_send.at[pl.ds(0, 31 * 32), :], send_sem.at[10])
    wait_bytes(squares.at[pl.ds(0, 3)], send_sem.at[11])

    @pl.when(me < NC - 1)
    def _():
        for which, stream in enumerate(streams):
            wait_bytes(stream.at[pl.ds(TOK - 16, 16), :], halo_send.at[which])


def shards(
    queries, key_vectors, stream_gate, stream_key, stream_value,
    short_filter, long_filter, skip_gain, out_gain,
):
    vmem = pl.BlockSpec(memory_space=pltpu.VMEM)
    flat = pltpu.VMEM((NC * PIECE, TOK), BF16)
    dma = pltpu.SemaphoreType.DMA
    shape = jax.ShapeDtypeStruct(stream_gate.shape, BF16)
    return pl.pallas_call(
        kernel,
        out_shape=(shape, shape),
        in_specs=[vmem] * 14,
        out_specs=(vmem, vmem),
        scratch_shapes=[
            pltpu.VMEM((3, 16, 1024), BF16),
            flat, flat, flat, flat, flat, flat,
            pltpu.VMEM((PIECE, NC * TOK), BF16),
            flat,
            pltpu.VMEM((NC * PIECE, TOK), F32),
            pltpu.VMEM((NC * PIECE, 2 * TOK), BF16),
            pltpu.VMEM((NC * PIECE, 2 * TOK), F32),
            pltpu.VMEM((NC * PIECE, 2 * TOK), F32),
            pltpu.VMEM((DH, DH), F32),
            pltpu.VMEM((2048, DH), BF16),
            pltpu.VMEM((4096, DH), BF16),
            pltpu.VMEM((DH, 4096), BF16),
            pltpu.VMEM((4096, QB), F32),
            pltpu.VMEM((36 * SPAN, QB), BF16),
            pltpu.VMEM((16, QB), F32),
            pltpu.VMEM((16, QB), F32),
            pltpu.VMEM((8, DH, 128), F32),
            pltpu.VMEM((8, DH, 128), BF16),
            pltpu.VMEM((8, DH, 128), BF16),
            flat,
            pltpu.VMEM((TOK, 1024), BF16),
            pltpu.VMEM((4, 8, TOK), F32),
            dma((12,)), dma((12,)), dma((3,)), dma((3,)), dma((8,)), dma((8,)),
        ],
        compiler_params=pltpu.CompilerParams(
            collective_id=0, has_side_effects=True, vmem_limit_bytes=48 * 2**20
        ),
    )(
        queries, key_vectors, stream_gate, stream_key, stream_value, short_filter, long_filter,
        skip_gain.reshape(8, DH), out_gain.reshape(1, 1024), *dft_constants(),
    )


def solution(mesh):
    in_specs = (
        P("ctx", "tp"),
        P("ctx", "tp"),
        P("ctx", "tp"),
        P("ctx", "tp"),
        P("ctx", "tp"),
        P(None, None, "tp"),
        P("tp", "ctx"),
        P("tp"),
        P("tp"),
    )
    out_specs = (P("ctx", "tp"), P("ctx", "tp"))
    return jax.shard_map(shards, mesh=mesh, in_specs=in_specs, out_specs=out_specs, check_vma=False)
```

```python
import math

import jax
import jax.numpy as jnp
import numpy as np
from jax import lax
from jax.experimental import pallas as pl
from jax.experimental.pallas import tpu as pltpu
from jax.sharding import PartitionSpec as P

DH = 128
HC = 4096
NC = 64
TOK = 128
PIECE = 16
F32 = jnp.float32
BF16 = jnp.bfloat16
SPAN = 512
QB = 256
LOW = -1e30
SCALE = math.log2(math.e) / math.sqrt(DH)


def block_of(dev):
    return (dev // 2) % 8 * 8 + dev // 16 * 2 + dev % 2


def slot_of(dev):
    return dev % 2 * 32 + dev // 2


def dft_constants():
    slots = np.arange(NC)
    first = (2 * (slots % 32) + slots // 32).astype(np.float64)
    freq = np.arange(NC) + 0.25
    inner = np.arange(TOK)
    outer = 2 * np.pi * freq[:, None] * first[None, :] / NC
    turn = 2 * np.pi * freq[:, None] * inner[None, :] / (NC * TOK)
    mix = 2 * np.pi * (inner[:, None] * inner[None, :] % TOK) / TOK
    cos, sin = np.cos(mix), np.sin(mix)
    outer_in = np.concatenate([np.cos(outer), np.sin(outer)], axis=0)
    outer_out = np.concatenate([np.cos(outer), np.sin(outer)], axis=0).T / (NC * TOK)
    inner_in = np.block([[cos, sin], [-sin, cos]])
    inner_out = np.block([[cos, -sin], [sin, cos]])
    turns = np.stack([np.cos(turn), np.sin(turn)])
    return (
        jnp.asarray(outer_in, BF16),
        jnp.asarray(turns, F32),
        jnp.asarray(inner_in, BF16),
        jnp.asarray(inner_out, BF16),
        jnp.asarray(outer_out, BF16),
    )


def rows16(index):
    return pl.ds(pl.multiple_of(index * PIECE, PIECE), PIECE)


def remote(src, dst, send_sem, recv_sem, dev):
    return pltpu.make_async_remote_copy(
        src_ref=src,
        dst_ref=dst,
        send_sem=send_sem,
        recv_sem=recv_sem,
        device_id={"ctx": dev},
        device_id_type=pl.DeviceIdType.MESH,
    )


def remote_tp(src, dst, send_sem, recv_sem, dev):
    return pltpu.make_async_remote_copy(
        src_ref=src,
        dst_ref=dst,
        send_sem=send_sem,
        recv_sem=recv_sem,
        device_id={"tp": dev},
        device_id_type=pl.DeviceIdType.MESH,
    )


def wait_bytes(ref, sem):
    pltpu.make_async_copy(ref, ref, sem).wait()


def mix_taps(stream, halo, taps, which, cols):
    values = stream[:, cols].astype(F32)
    behind = halo[which, :, cols].astype(F32)
    row = lax.broadcasted_iota(jnp.int32, values.shape, 0)
    once = jnp.where(row == 0, behind[15:16], pltpu.roll(values, 1, 0))
    twice = pltpu.roll(values, 2, 0)
    twice = jnp.where(row == 0, behind[14:15], jnp.where(row == 1, behind[15:16], twice))
    mixed = (
        taps[which, 0:1, cols] * values
        + taps[which, 1:2, cols] * once
        + taps[which, 2:3, cols] * twice
    )
    return mixed.astype(BF16)


def spectrum(recv, wide, half, spec, outer_in, turns, inner_in):
    wide[...] = recv[...].astype(F32)
    turn_re, turn_im = turns[0], turns[1]
    for chan in range(0, PIECE, 2):
        pair = [wide[pl.ds(chan + k, NC, stride=PIECE), :].astype(BF16) for k in range(2)]
        both = jnp.dot(outer_in[...], jnp.concatenate(pair, axis=1), preferred_element_type=F32)
        for k in range(2):
            re, im = both[:NC, k * TOK : (k + 1) * TOK], both[NC:, k * TOK : (k + 1) * TOK]
            at = pl.ds((chan + k) * NC, NC)
            half[at, 0:TOK] = (re * turn_re - im * turn_im).astype(BF16)
            half[at, TOK : 2 * TOK] = (re * turn_im + im * turn_re).astype(BF16)
    for part in range(4):
        at = pl.ds(part * 256, 256)
        spec[at, :] = jnp.dot(half[at, :], inner_in[...], preferred_element_type=F32)


def multiply_back(spec_x, spec_h, half, wide, turns, inner_out, outer_out):
    turn_re, turn_im = turns[0], turns[1]
    for part in range(4):
        at = pl.ds(part * 256, 256)
        xr, xi = spec_x[at, 0:TOK], spec_x[at, TOK : 2 * TOK]
        hr, hi = spec_h[at, 0:TOK], spec_h[at, TOK : 2 * TOK]
        half[at, 0:TOK] = (xr * hr - xi * hi).astype(BF16)
        half[at, TOK : 2 * TOK] = (xr * hi + xi * hr).astype(BF16)
    for chan in range(0, PIECE, 2):
        back = jnp.dot(
            half[pl.ds(chan * NC, 2 * NC), :], inner_out[...], preferred_element_type=F32
        )
        pair = []
        for k in range(2):
            re, im = back[k * NC : (k + 1) * NC, :TOK], back[k * NC : (k + 1) * NC, TOK:]
            turned = jnp.concatenate(
                [re * turn_re + im * turn_im, im * turn_re - re * turn_im], axis=0
            )
            pair.append(turned.astype(BF16))
        both = jnp.dot(outer_out[...], jnp.concatenate(pair, axis=1), preferred_element_type=F32)
        for k in range(2):
            wide[pl.ds(chan + k, NC, stride=PIECE), :] = both[:, k * TOK : (k + 1) * TOK]


def attend_scores(
    block, core, across, queries, keys, scores, weights, stats
):
    own = queries[pl.ds(pl.multiple_of(core * 1024 + block * 128, 128), 128), :]
    other = queries[pl.ds(pl.multiple_of((1 - core) * 1024 + block * 128, 128), 128), :]
    both = jnp.concatenate([own, other], axis=0)

    def chunk_rows(chunk):
        return pl.ds(pl.multiple_of(chunk * SPAN, SPAN), SPAN)

    def chunk_scores(chunk):
        return lax.dot_general(
            keys[chunk_rows(chunk), :],
            both,
            (((1,), (1,)), ((), ())),
            preferred_element_type=F32,
        )

    def first(chunk, run_max):
        here = chunk_scores(chunk)
        scores[chunk_rows(chunk), :] = here
        return jnp.maximum(run_max, here.reshape(SPAN // 8, 8, QB).max(axis=0))

    run_max = lax.fori_loop(0, block, first, jnp.full((8, QB), LOW, F32))
    row = lax.broadcasted_iota(jnp.int32, (SPAN, QB), 0)
    lane = lax.broadcasted_iota(jnp.int32, (SPAN, QB), 1)
    key_pos = row // 128 * 256 + core * 128 + row % 128
    parity = jnp.where(lane < 128, core, 1 - core)
    query_pos = lane % 128 // 32 * 256 + parity * 128 + across * 32 + lane % 32
    here = jnp.where(key_pos <= query_pos, chunk_scores(block), LOW)
    scores[chunk_rows(block), :] = here
    run_max = jnp.maximum(run_max, here.reshape(SPAN // 8, 8, QB).max(axis=0))
    top = run_max.max(axis=0, keepdims=True) * SCALE
    base = block * (block + 1) // 2

    def second(chunk, total):
        terms = jnp.exp2(scores[chunk_rows(chunk), :] * SCALE - top)
        weights[chunk_rows(base + chunk), :] = terms.astype(BF16)
        return total + terms.reshape(SPAN // 8, 8, QB).sum(axis=0)

    total = lax.fori_loop(0, block + 1, second, jnp.zeros((8, QB), F32))
    stats[pl.ds(block, 1), :] = top
    stats[pl.ds(8 + block, 1), :] = total.sum(axis=0, keepdims=True)


def value_chunk(chunk, values, weights, totals):
    lanes = slice(chunk * 1024, (chunk + 1) * 1024)
    for block in range(2 * chunk, 8):
        first = (block * (block + 1) // 2 + 2 * chunk) * SPAN
        reach = SPAN if block == 2 * chunk else 2 * SPAN
        add = jnp.dot(
            values[:, lanes][:, :reach],
            weights[first : first + reach, :],
            preferred_element_type=F32,
        )
        totals[block] = add if chunk == 0 else totals[block] + add


def share_factor(block, stats, other_stats):
    top, count = stats[pl.ds(block, 1), :], stats[pl.ds(8 + block, 1), :]
    swap = lambda v: jnp.concatenate([v[:, 128:], v[:, :128]], axis=1)
    other_top = swap(other_stats[pl.ds(block, 1), :])
    other_count = swap(other_stats[pl.ds(8 + block, 1), :])
    both_top = jnp.maximum(top, other_top)
    mine = jnp.exp2(top - both_top)
    whole = mine * count + jnp.exp2(other_top - both_top) * other_count
    return mine / whole


def kernel(
    queries, key_vectors, gate_hbm, key_hbm, value_hbm,
    taps_hbm, filter_hbm, skip_hbm, gain_hbm,
    outer_in_hbm, turns_hbm, inner_in_hbm, inner_out_hbm, outer_out_hbm,
    hyena_out, attn_out,
    stream_gate, stream_key, stream_value, taps, long_filter, skip_gain, out_gain,
    outer_in, turns, inner_in, inner_out, outer_out,
    halo, filt_send, prod_send, gate_send, filt_recv, prod_recv, gate_recv,
    hyena, home, wide, half, spec_x, spec_h, column,
    query_all, key_all, value_all, scores, weights, stats, other_stats,
    totals, own_part, part_send, part_recv, att_send, att_home, squares,
    send_sem, recv_sem, halo_send, halo_recv, part_out, part_in,
    load_sem, value_out_sem, value_in_sem,
):
    me = lax.axis_index("ctx")
    tp = lax.axis_index("tp")
    across, depth, core = me // 16, (me // 2) % 8, me % 2
    pair, sibling = me // 2, me + 1 - 2 * core
    member = across * 2 + core
    my_block, my_slot = block_of(me), slot_of(me)
    barrier = pltpu.get_barrier_semaphore()

    def greet(step, unused):
        pl.semaphore_signal(
            barrier,
            inc=1,
            device_id={"ctx": lax.rem(me + step, NC)},
            device_id_type=pl.DeviceIdType.MESH,
        )
        return unused

    lax.fori_loop(1, NC, greet, 0)
    for step in range(1, 4):
        pl.semaphore_signal(
            barrier,
            inc=1,
            device_id={"tp": lax.rem(tp + step, 4)},
            device_id_type=pl.DeviceIdType.MESH,
        )
    loads = [
        pltpu.make_async_copy(src, dst, load_sem.at[index])
        for index, (src, dst) in enumerate(
            (
                (filter_hbm, long_filter),
                (taps_hbm, taps),
                (key_hbm, stream_key),
                (value_hbm, stream_value),
                (gate_hbm, stream_gate),
                (outer_in_hbm, outer_in),
                (turns_hbm, turns),
                (inner_in_hbm, inner_in),
                (inner_out_hbm, inner_out),
                (outer_out_hbm, outer_out),
                (skip_hbm, skip_gain),
                (gain_hbm, out_gain),
            )
        )
    ]
    key_rows = pl.ds(pl.multiple_of(pair * 128, 128), 128)
    query_rows = pl.ds(pl.multiple_of(core * 1024 + pair * 32, 32), 32)
    across_rows = pl.ds(pl.multiple_of(across * 32, 32), 32)
    my_cols = pl.ds(pl.multiple_of(depth * DH, DH), DH)
    loads.append(
        pltpu.make_async_copy(key_vectors.at[:, my_cols], key_all.at[key_rows, :], load_sem.at[12])
    )
    loads.append(
        pltpu.make_async_copy(
            queries.at[across_rows, my_cols], query_all.at[query_rows, :], load_sem.at[13]
        )
    )
    for load in loads:
        load.start()

    @pl.when(me == 0)
    def _():
        halo[...] = jnp.zeros_like(halo)

    loads[0].wait()
    filt_send[...] = long_filter[...].astype(BF16)
    pl.semaphore_wait(barrier, NC - 1 + 3)

    streams = (gate_hbm, key_hbm, value_hbm)

    @pl.when(me < NC - 1)
    def _():
        for which, stream in enumerate(streams):
            remote(
                stream.at[pl.ds(TOK - 16, 16), :],
                halo.at[which],
                halo_send.at[which],
                halo_recv.at[which],
                me + 1,
            ).start()

    def key_out(step, unused):
        head = lax.rem(depth + step, 8)
        remote(
            key_vectors.at[:, pl.ds(pl.multiple_of(head * DH, DH), DH)],
            key_all.at[key_rows, :],
            send_sem.at[4],
            recv_sem.at[4],
            across * 16 + head * 2 + core,
        ).start()
        return unused

    lax.fori_loop(1, 8, key_out, 0)

    def scatter(send, recv, index):
        def one(step, unused):
            dev = lax.rem(me + step, NC)
            remote(
                send.at[rows16(block_of(dev)), :],
                recv.at[rows16(my_slot), :],
                send_sem.at[index],
                recv_sem.at[index],
                dev,
            ).start()
            return unused

        lax.fori_loop(1, NC, one, 0)
        recv[rows16(my_slot), :] = send[rows16(my_block), :]

    rest = pl.ds(0, (NC - 1) * PIECE)
    scatter(filt_send, filt_recv, 0)

    for load in loads[1:5]:
        load.wait()

    @pl.when(me > 0)
    def _():
        for which in range(3):
            wait_bytes(halo.at[which], halo_recv.at[which])

    def columns(head, unused):
        cols = pl.ds(pl.multiple_of(head * DH, DH), DH)
        key_feat = mix_taps(stream_key, halo, taps, 1, cols)
        value_feat = mix_taps(stream_value, halo, taps, 2, cols)
        product = key_feat.astype(F32) * value_feat.astype(F32)
        prod_send[cols, :] = product.T.astype(BF16)
        return unused

    lax.fori_loop(0, 8, columns, 0)
    scatter(prod_send, prod_recv, 1)

    def gate_columns(head, unused):
        cols = pl.ds(pl.multiple_of(head * DH, DH), DH)
        gate_feat = mix_taps(stream_gate, halo, taps, 0, cols)
        gate_send[cols, :] = gate_feat.astype(F32).T.astype(BF16)
        return unused

    lax.fori_loop(0, 8, gate_columns, 0)
    scatter(gate_send, gate_recv, 2)

    def query_out(step, unused):
        goal = lax.rem(pair + step, 32)
        remote(
            queries.at[
                pl.ds(pl.multiple_of(goal // 8 * 32, 32), 32),
                pl.ds(pl.multiple_of(goal % 8 * DH, DH), DH),
            ],
            query_all.at[query_rows, :],
            send_sem.at[5],
            recv_sem.at[5],
            goal * 2 + core,
        ).start()
        return unused

    lax.fori_loop(1, 32, query_out, 0)

    for load in loads[5:]:
        load.wait()
    wait_bytes(key_all.at[pl.ds(0, 7 * 128), :], recv_sem.at[4])
    keys_here = pl.ds(pl.multiple_of(across * 1024, 1024), 1024)

    def key_on(step, unused):
        remote(
            key_all.at[keys_here, :],
            key_all.at[keys_here, :],
            send_sem.at[6],
            recv_sem.at[6],
            lax.rem(across + step, 4) * 16 + depth * 2 + core,
        ).start()
        return unused

    lax.fori_loop(1, 4, key_on, 0)

    head_row = skip_gain[pl.ds(depth, 1), :]
    column[...] = jnp.broadcast_to(head_row, (DH, DH)).T
    skip_tile = column[rows16(my_block % 8), :]

    wait_bytes(filt_recv.at[rest, :], recv_sem.at[0])
    spectrum(filt_recv, wide, half, spec_h, outer_in, turns, inner_in)
    wait_bytes(prod_recv.at[rest, :], recv_sem.at[1])

    spectrum(prod_recv, wide, half, spec_x, outer_in, turns, inner_in)
    multiply_back(spec_x, spec_h, half, wide, turns, inner_out, outer_out)
    wait_bytes(gate_recv.at[rest, :], recv_sem.at[2])

    def gated(slot, unused):
        at = rows16(slot)
        inner = wide[at, :] + skip_tile * prod_recv[at, :].astype(F32)
        lanes = pl.ds(pl.multiple_of(slot * TOK, TOK), TOK)
        hyena[:, lanes] = (gate_recv[at, :].astype(F32) * inner).astype(BF16)
        return unused

    for chunk in range(4):
        lax.fori_loop(chunk * 8, chunk * 8 + 8, gated, 0, unroll=True)
        lax.fori_loop(32 + chunk * 8, 32 + chunk * 8 + 8, gated, 0, unroll=True)

        def value_out(step, unused):
            goal = lax.rem(member + step, 8)
            lanes = pl.ds(pl.multiple_of(goal % 2 * 4096 + chunk * 1024, 1024), 1024)
            remote(
                hyena.at[:, lanes],
                value_all.at[rows16(member), pl.ds(chunk * 1024, 1024)],
                value_out_sem.at[chunk],
                value_in_sem.at[chunk],
                goal // 2 * 16 + depth * 2 + goal % 2,
            ).start()
            return unused

        lax.fori_loop(1, 8, value_out, 0)
        lanes = pl.ds(pl.multiple_of(core * 4096 + chunk * 1024, 1024), 1024)
        value_all[rows16(member), pl.ds(chunk * 1024, 1024)] = hyena[:, lanes]

    def go_home(step, unused):
        dev = lax.rem(me + step, NC)
        remote(
            hyena.at[:, pl.ds(pl.multiple_of(slot_of(dev) * TOK, TOK), TOK)],
            home.at[rows16(my_block), :],
            send_sem.at[3],
            recv_sem.at[3],
            dev,
        ).start()
        return unused

    lax.fori_loop(1, NC, go_home, 0)
    home[rows16(my_block), :] = hyena[:, pl.ds(pl.multiple_of(my_slot * TOK, TOK), TOK)]

    wait_bytes(query_all.at[pl.ds(0, 31 * 32), :], recv_sem.at[5])
    queries_here = pl.ds(pl.multiple_of(core * 1024, 1024), 1024)
    query_on = remote(
        query_all.at[queries_here, :],
        query_all.at[queries_here, :],
        send_sem.at[7],
        recv_sem.at[7],
        sibling,
    )
    query_on.start()
    wait_bytes(key_all.at[pl.ds(0, 3 * 1024), :], recv_sem.at[6])
    query_on.wait_recv()

    def scoring(step, unused):
        block = lax.rem(depth + step, 8)
        attend_scores(
            block, core, across, query_all, key_all, scores, weights, stats
        )
        return unused

    lax.fori_loop(0, 8, scoring, 0)
    stats_out = remote(stats, other_stats, send_sem.at[9], recv_sem.at[9], sibling)
    stats_out.start()

    for chunk in range(4):
        wait_bytes(
            value_all.at[pl.ds(0, 7 * PIECE), pl.ds(chunk * 1024, 1024)], value_in_sem.at[chunk]
        )
        value_chunk(chunk, value_all, weights, totals)
    stats_out.wait_recv()

    def part_copy(block):
        return remote(
            part_send.at[block],
            part_recv.at[block],
            part_out.at[block],
            part_in.at[block],
            sibling,
        )

    def settle(block):
        part_copy(block).wait_recv()
        whole = own_part[block] + part_recv[block].astype(F32)
        att_send[pl.ds(pl.multiple_of(block * 128, 128), 128), :] = whole.T.astype(BF16)

        for k in range(4):
            goal = block * 4 + k
            rows = pl.ds(pl.multiple_of(goal * 32, 32), 32)

            @pl.when(goal != pair)
            def _():
                remote(
                    att_send.at[rows, :],
                    att_home.at[across_rows, my_cols],
                    send_sem.at[10],
                    recv_sem.at[10],
                    goal * 2 + core,
                ).start()

            @pl.when(goal == pair)
            def _():
                att_home[across_rows, my_cols] = att_send[rows, :]

    def sharing(step, unused):
        block = lax.rem(depth + step, 8)
        total = totals[block] * share_factor(block, stats, other_stats)
        own_part[block] = total[:, :128]
        part_send[block] = total[:, 128:].astype(BF16)
        part_copy(block).start()
        return unused

    lax.fori_loop(0, 8, sharing, 0)

    def settling(step, unused):
        settle(lax.rem(depth + step, 8))
        return unused

    lax.fori_loop(0, 8, settling, 0)

    wait_bytes(home.at[rest, :], recv_sem.at[3])

    def finish(head, unused):
        cols = pl.ds(pl.multiple_of(head * DH, DH), DH)
        hyena_out[:, cols] = home[cols, :].astype(F32).T.astype(BF16)
        return unused

    lax.fori_loop(0, 8, finish, 0)

    wait_bytes(att_send.at[pl.ds(0, 31 * 32), :], recv_sem.at[10])
    summed = jnp.zeros((TOK, DH), F32)
    for head in range(8):
        part = att_home[:, head * DH : (head + 1) * DH].astype(F32)
        summed = summed + part * part
    squares[tp] = jnp.broadcast_to(summed.T.sum(axis=0, keepdims=True), (8, TOK))
    for step in range(1, 4):
        remote_tp(
            squares.at[tp],
            squares.at[tp],
            send_sem.at[11],
            recv_sem.at[11],
            lax.rem(tp + step, 4),
        ).start()
    wait_bytes(squares.at[pl.ds(0, 3)], recv_sem.at[11])
    mean = (squares[0] + squares[1] + squares[2] + squares[3]) * (1.0 / HC)
    inverse = jnp.broadcast_to(lax.rsqrt(mean + 1e-05)[0:1, :], (TOK, TOK)).T
    for head in range(8):
        cols = slice(head * DH, (head + 1) * DH)
        part = att_home[:, cols].astype(F32)
        attn_out[:, cols] = (part * inverse * out_gain[0:1, cols]).astype(BF16)

    for index, send in enumerate((filt_send, prod_send, gate_send, home)):
        wait_bytes(send.at[rest, :], send_sem.at[index])
    wait_bytes(key_all.at[pl.ds(0, 7 * 128), :], send_sem.at[4])
    wait_bytes(query_all.at[pl.ds(0, 31 * 32), :], send_sem.at[5])
    wait_bytes(key_all.at[pl.ds(0, 3 * 1024), :], send_sem.at[6])
    query_on.wait_send()
    for chunk in range(4):
        wait_bytes(
            value_all.at[pl.ds(0, 7 * PIECE), pl.ds(chunk * 1024, 1024)], value_out_sem.at[chunk]
        )
    stats_out.wait_send()
    for block in range(8):
        part_copy(block).wait_send()
    wait_bytes(att_send.at[pl.ds(0, 31 * 32), :], send_sem.at[10])
    wait_bytes(squares.at[pl.ds(0, 3)], send_sem.at[11])

    @pl.when(me < NC - 1)
    def _():
        for which, stream in enumerate(streams):
            wait_bytes(stream.at[pl.ds(TOK - 16, 16), :], halo_send.at[which])


def shards(
    queries, key_vectors, stream_gate, stream_key, stream_value,
    short_filter, long_filter, skip_gain, out_gain,
):
    vmem = pl.BlockSpec(memory_space=pltpu.VMEM)
    flat = pltpu.VMEM((NC * PIECE, TOK), BF16)
    dma = pltpu.SemaphoreType.DMA
    constants = dft_constants()
    shape = jax.ShapeDtypeStruct(stream_gate.shape, BF16)
    return pl.pallas_call(
        kernel,
        out_shape=(shape, shape),
        in_specs=[pl.BlockSpec(memory_space=pltpu.HBM)] * 14,
        out_specs=(vmem, vmem),
        scratch_shapes=[
            *[pltpu.VMEM((TOK, 1024), BF16)] * 3,
            pltpu.VMEM((3, 3, 1024), F32),
            pltpu.VMEM((1024, TOK), F32),
            pltpu.VMEM((8, DH), F32),
            pltpu.VMEM((1, 1024), F32),
            *[pltpu.VMEM(c.shape, c.dtype) for c in constants],
            pltpu.VMEM((3, 16, 1024), BF16),
            flat, flat, flat, flat, flat, flat,
            pltpu.VMEM((PIECE, NC * TOK), BF16),
            flat,
            pltpu.VMEM((NC * PIECE, TOK), F32),
            pltpu.VMEM((NC * PIECE, 2 * TOK), BF16),
            pltpu.VMEM((NC * PIECE, 2 * TOK), F32),
            pltpu.VMEM((NC * PIECE, 2 * TOK), F32),
            pltpu.VMEM((DH, DH), F32),
            pltpu.VMEM((2048, DH), BF16),
            pltpu.VMEM((4096, DH), BF16),
            pltpu.VMEM((DH, 4096), BF16),
            pltpu.VMEM((4096, QB), F32),
            pltpu.VMEM((36 * SPAN, QB), BF16),
            pltpu.VMEM((16, QB), F32),
            pltpu.VMEM((16, QB), F32),
            pltpu.VMEM((8, DH, QB), F32),
            pltpu.VMEM((8, DH, 128), F32),
            pltpu.VMEM((8, DH, 128), BF16),
            pltpu.VMEM((8, DH, 128), BF16),
            flat,
            pltpu.VMEM((TOK, 1024), BF16),
            pltpu.VMEM((4, 8, TOK), F32),
            dma((12,)), dma((12,)), dma((3,)), dma((3,)), dma((8,)), dma((8,)),
            dma((14,)), dma((4,)), dma((4,)),
        ],
        compiler_params=pltpu.CompilerParams(
            collective_id=0, has_side_effects=True, vmem_limit_bytes=48 * 2**20
        ),
    )(
        queries, key_vectors, stream_gate, stream_key, stream_value, short_filter, long_filter,
        skip_gain.reshape(8, DH), out_gain.reshape(1, 1024), *constants,
    )


def solution(mesh):
    in_specs = (
        P("ctx", "tp"),
        P("ctx", "tp"),
        P("ctx", "tp"),
        P("ctx", "tp"),
        P("ctx", "tp"),
        P(None, None, "tp"),
        P("tp", "ctx"),
        P("tp"),
        P("tp"),
    )
    out_specs = (P("ctx", "tp"), P("ctx", "tp"))
    return jax.shard_map(shards, mesh=mesh, in_specs=in_specs, out_specs=out_specs, check_vma=False)
```

```python
import math

import jax
import jax.numpy as jnp
import numpy as np
from jax import lax
from jax.experimental import pallas as pl
from jax.experimental.pallas import tpu as pltpu
from jax.sharding import PartitionSpec as P

DH = 128
HC = 4096
NC = 64
TOK = 128
PIECE = 16
F32 = jnp.float32
BF16 = jnp.bfloat16
SPAN = 512
QB = 256
LOW = -1e30
SCALE = math.log2(math.e) / math.sqrt(DH)


def block_of(dev):
    return (dev // 2) % 8 * 8 + dev // 16 * 2 + dev % 2


def slot_of(dev):
    return dev % 2 * 32 + dev // 2


def dft_constants():
    slots = np.arange(NC)
    first = (2 * (slots % 32) + slots // 32).astype(np.float64)
    freq = np.arange(NC) + 0.25
    inner = np.arange(TOK)
    outer = 2 * np.pi * freq[:, None] * first[None, :] / NC
    turn = 2 * np.pi * freq[:, None] * inner[None, :] / (NC * TOK)
    mix = 2 * np.pi * (inner[:, None] * inner[None, :] % TOK) / TOK
    cos, sin = np.cos(mix), np.sin(mix)
    outer_in = np.concatenate([np.cos(outer), np.sin(outer)], axis=0)
    outer_out = np.concatenate([np.cos(outer), np.sin(outer)], axis=0).T / (NC * TOK)
    inner_in = np.block([[cos, sin], [-sin, cos]])
    inner_out = np.block([[cos, -sin], [sin, cos]])
    turns = np.stack([np.cos(turn), np.sin(turn)])
    return (
        jnp.asarray(outer_in, BF16),
        jnp.asarray(turns, F32),
        jnp.asarray(inner_in, BF16),
        jnp.asarray(inner_out, BF16),
        jnp.asarray(outer_out, BF16),
    )


def rows16(index):
    return pl.ds(pl.multiple_of(index * PIECE, PIECE), PIECE)


def remote(src, dst, send_sem, recv_sem, dev):
    return pltpu.make_async_remote_copy(
        src_ref=src,
        dst_ref=dst,
        send_sem=send_sem,
        recv_sem=recv_sem,
        device_id={"ctx": dev},
        device_id_type=pl.DeviceIdType.MESH,
    )


def remote_tp(src, dst, send_sem, recv_sem, dev):
    return pltpu.make_async_remote_copy(
        src_ref=src,
        dst_ref=dst,
        send_sem=send_sem,
        recv_sem=recv_sem,
        device_id={"tp": dev},
        device_id_type=pl.DeviceIdType.MESH,
    )


def wait_bytes(ref, sem):
    pltpu.make_async_copy(ref, ref, sem).wait()


def mix_taps(stream, halo, taps, which, cols):
    values = stream[:, cols].astype(F32)
    behind = halo[which, :, cols].astype(F32)
    row = lax.broadcasted_iota(jnp.int32, values.shape, 0)
    once = jnp.where(row == 0, behind[15:16], pltpu.roll(values, 1, 0))
    twice = pltpu.roll(values, 2, 0)
    twice = jnp.where(row == 0, behind[14:15], jnp.where(row == 1, behind[15:16], twice))
    mixed = (
        taps[which, 0:1, cols] * values
        + taps[which, 1:2, cols] * once
        + taps[which, 2:3, cols] * twice
    )
    return mixed.astype(BF16)


def spectrum(recv, wide, half, spec, outer_in, turns, inner_in):
    wide[...] = recv[...].astype(F32)
    turn_re, turn_im = turns[0], turns[1]
    for chan in range(0, PIECE, 2):
        pair = [wide[pl.ds(chan + k, NC, stride=PIECE), :].astype(BF16) for k in range(2)]
        both = jnp.dot(outer_in[...], jnp.concatenate(pair, axis=1), preferred_element_type=F32)
        for k in range(2):
            re, im = both[:NC, k * TOK : (k + 1) * TOK], both[NC:, k * TOK : (k + 1) * TOK]
            at = pl.ds((chan + k) * NC, NC)
            half[at, 0:TOK] = (re * turn_re - im * turn_im).astype(BF16)
            half[at, TOK : 2 * TOK] = (re * turn_im + im * turn_re).astype(BF16)
    for part in range(4):
        at = pl.ds(part * 256, 256)
        spec[at, :] = jnp.dot(half[at, :], inner_in[...], preferred_element_type=F32)


def multiply_back(spec_x, spec_h, half, wide, turns, inner_out, outer_out):
    turn_re, turn_im = turns[0], turns[1]
    for part in range(4):
        at = pl.ds(part * 256, 256)
        xr, xi = spec_x[at, 0:TOK], spec_x[at, TOK : 2 * TOK]
        hr, hi = spec_h[at, 0:TOK], spec_h[at, TOK : 2 * TOK]
        half[at, 0:TOK] = (xr * hr - xi * hi).astype(BF16)
        half[at, TOK : 2 * TOK] = (xr * hi + xi * hr).astype(BF16)
    for chan in range(0, PIECE, 2):
        back = jnp.dot(
            half[pl.ds(chan * NC, 2 * NC), :], inner_out[...], preferred_element_type=F32
        )
        pair = []
        for k in range(2):
            re, im = back[k * NC : (k + 1) * NC, :TOK], back[k * NC : (k + 1) * NC, TOK:]
            turned = jnp.concatenate(
                [re * turn_re + im * turn_im, im * turn_re - re * turn_im], axis=0
            )
            pair.append(turned.astype(BF16))
        both = jnp.dot(outer_out[...], jnp.concatenate(pair, axis=1), preferred_element_type=F32)
        for k in range(2):
            wide[pl.ds(chan + k, NC, stride=PIECE), :] = both[:, k * TOK : (k + 1) * TOK]


def span(chunk):
    return pl.ds(pl.multiple_of(chunk * SPAN, SPAN), SPAN)


def visible_bias(core, across):
    row = lax.broadcasted_iota(jnp.int32, (SPAN, QB), 0)
    lane = lax.broadcasted_iota(jnp.int32, (SPAN, QB), 1)
    key_pos = row // 128 * 256 + core * 128 + row % 128
    parity = jnp.where(lane < 128, core, 1 - core)
    query_pos = lane % 128 // 32 * 256 + parity * 128 + across * 32 + lane % 32
    return jnp.where(key_pos <= query_pos, 0.0, LOW)


def attend_scores(core, queries, keys, score_slots, bias, weights, stats):
    def both_halves(block):
        own = queries[pl.ds(pl.multiple_of(core * 1024 + block * 128, 128), 128), :]
        other = queries[pl.ds(pl.multiple_of((1 - core) * 1024 + block * 128, 128), 128), :]
        return jnp.concatenate([own, other], axis=0)

    def score(block, chunk, run_max, masked):
        here = lax.dot_general(
            keys[span(chunk), :],
            both_halves(block),
            (((1,), (1,)), ((), ())),
            preferred_element_type=F32,
        )
        if masked:
            here = here + bias[...]
        score_slots[block % 2][span(chunk), :] = here
        return jnp.maximum(run_max, here.reshape(SPAN // 8, 8, QB).max(axis=0))

    def weigh(block, chunk, top, total):
        terms = jnp.exp2(score_slots[block % 2][span(chunk), :] * SCALE - top)
        weights[span(block * (block + 1) // 2 + chunk), :] = terms.astype(BF16)
        return total + terms.reshape(SPAN // 8, 8, QB).sum(axis=0)

    lowest = jnp.full((8, QB), LOW, F32)
    none = jnp.zeros((8, QB), F32)
    run_max = lax.fori_loop(0, 7, lambda chunk, run: score(7, chunk, run, False), lowest)
    run_max = score(7, 7, run_max, True)
    for block in range(7, -1, -1):
        top = run_max.max(axis=0, keepdims=True) * SCALE

        def beside(chunk, carry, block=block, top=top):
            total, run = carry
            return (weigh(block, chunk, top, total), score(block - 1, chunk, run, False))

        total, run_max = lax.fori_loop(0, block - 1, beside, (none, lowest))
        if block > 0:
            total = weigh(block, block - 1, top, total)
            run_max = score(block - 1, block - 1, run_max, True)
        total = weigh(block, block, top, total)
        stats[block : block + 1, :] = top
        stats[8 + block : 9 + block, :] = total.sum(axis=0, keepdims=True)


def value_chunk(chunk, values, weights, totals):
    lanes = slice(chunk * 1024, (chunk + 1) * 1024)
    for block in range(2 * chunk, 8):
        first = (block * (block + 1) // 2 + 2 * chunk) * SPAN
        reach = SPAN if block == 2 * chunk else 2 * SPAN
        add = jnp.dot(
            values[:, lanes][:, :reach],
            weights[first : first + reach, :],
            preferred_element_type=F32,
        )
        totals[block] = add if chunk == 0 else totals[block] + add


def share_factor(block, stats, other_stats):
    top, count = stats[pl.ds(block, 1), :], stats[pl.ds(8 + block, 1), :]
    swap = lambda v: jnp.concatenate([v[:, 128:], v[:, :128]], axis=1)
    other_top = swap(other_stats[pl.ds(block, 1), :])
    other_count = swap(other_stats[pl.ds(8 + block, 1), :])
    both_top = jnp.maximum(top, other_top)
    mine = jnp.exp2(top - both_top)
    whole = mine * count + jnp.exp2(other_top - both_top) * other_count
    return mine / whole


def kernel(
    queries, key_vectors, gate_hbm, key_hbm, value_hbm,
    taps_hbm, filter_hbm, skip_hbm, gain_hbm,
    outer_in_hbm, turns_hbm, inner_in_hbm, inner_out_hbm, outer_out_hbm,
    hyena_out, attn_out,
    stream_gate, stream_key, stream_value, taps, long_filter, skip_gain, out_gain,
    outer_in, turns, inner_in, inner_out, outer_out,
    halo, filt_send, prod_send, gate_send, filt_recv, prod_recv, gate_recv,
    hyena, home, wide, half, spec_x, spec_h, column,
    query_all, key_all, value_all, scores_even, scores_odd, bias, weights, stats, other_stats,
    totals, own_part, part_send, part_recv, att_send, att_home, sum_own, sum_tp, sum_send, sum_home,
    send_sem, recv_sem, halo_send, halo_recv, part_out, part_in,
    load_sem, value_out_sem, value_in_sem,
):
    me = lax.axis_index("ctx")
    tp = lax.axis_index("tp")
    across, depth, core = me // 16, (me // 2) % 8, me % 2
    pair, sibling = me // 2, me + 1 - 2 * core
    member = across * 2 + core
    my_block, my_slot = block_of(me), slot_of(me)
    barrier = pltpu.get_barrier_semaphore()

    def greet(step, unused):
        pl.semaphore_signal(
            barrier,
            inc=1,
            device_id={"ctx": lax.rem(me + step, NC)},
            device_id_type=pl.DeviceIdType.MESH,
        )
        return unused

    lax.fori_loop(1, NC, greet, 0)
    for step in range(1, 4):
        pl.semaphore_signal(
            barrier,
            inc=1,
            device_id={"tp": lax.rem(tp + step, 4)},
            device_id_type=pl.DeviceIdType.MESH,
        )
    loads = [
        pltpu.make_async_copy(src, dst, load_sem.at[index])
        for index, (src, dst) in enumerate(
            (
                (filter_hbm, long_filter),
                (taps_hbm, taps),
                (key_hbm, stream_key),
                (value_hbm, stream_value),
                (gate_hbm, stream_gate),
                (outer_in_hbm, outer_in),
                (turns_hbm, turns),
                (inner_in_hbm, inner_in),
                (inner_out_hbm, inner_out),
                (outer_out_hbm, outer_out),
                (skip_hbm, skip_gain),
                (gain_hbm, out_gain),
            )
        )
    ]
    key_rows = pl.ds(pl.multiple_of(pair * 128, 128), 128)
    query_rows = pl.ds(pl.multiple_of(core * 1024 + pair * 32, 32), 32)
    across_rows = pl.ds(pl.multiple_of(across * 32, 32), 32)
    my_cols = pl.ds(pl.multiple_of(depth * DH, DH), DH)
    loads.append(
        pltpu.make_async_copy(key_vectors.at[:, my_cols], key_all.at[key_rows, :], load_sem.at[12])
    )
    loads.append(
        pltpu.make_async_copy(
            queries.at[across_rows, my_cols], query_all.at[query_rows, :], load_sem.at[13]
        )
    )
    for load in loads:
        load.start()

    @pl.when(me == 0)
    def _():
        halo[...] = jnp.zeros_like(halo)

    loads[0].wait()
    filt_send[...] = long_filter[...].astype(BF16)
    pl.semaphore_wait(barrier, NC - 1 + 3)

    streams = (gate_hbm, key_hbm, value_hbm)

    @pl.when(me < NC - 1)
    def _():
        for which, stream in enumerate(streams):
            remote(
                stream.at[pl.ds(TOK - 16, 16), :],
                halo.at[which],
                halo_send.at[which],
                halo_recv.at[which],
                me + 1,
            ).start()

    def key_out(step, unused):
        head = lax.rem(depth + step, 8)
        remote(
            key_vectors.at[:, pl.ds(pl.multiple_of(head * DH, DH), DH)],
            key_all.at[key_rows, :],
            send_sem.at[4],
            recv_sem.at[4],
            across * 16 + head * 2 + core,
        ).start()
        return unused

    lax.fori_loop(1, 8, key_out, 0)

    def scatter(send, recv, index):
        def one(step, unused):
            dev = lax.rem(me + step, NC)
            remote(
                send.at[rows16(block_of(dev)), :],
                recv.at[rows16(my_slot), :],
                send_sem.at[index],
                recv_sem.at[index],
                dev,
            ).start()
            return unused

        lax.fori_loop(1, NC, one, 0)
        recv[rows16(my_slot), :] = send[rows16(my_block), :]

    rest = pl.ds(0, (NC - 1) * PIECE)
    scatter(filt_send, filt_recv, 0)

    for load in loads[1:5]:
        load.wait()

    @pl.when(me > 0)
    def _():
        for which in range(3):
            wait_bytes(halo.at[which], halo_recv.at[which])

    def columns(head, unused):
        cols = pl.ds(pl.multiple_of(head * DH, DH), DH)
        key_feat = mix_taps(stream_key, halo, taps, 1, cols)
        value_feat = mix_taps(stream_value, halo, taps, 2, cols)
        product = key_feat.astype(F32) * value_feat.astype(F32)
        prod_send[cols, :] = product.T.astype(BF16)
        return unused

    lax.fori_loop(0, 8, columns, 0)
    scatter(prod_send, prod_recv, 1)

    def gate_columns(head, unused):
        cols = pl.ds(pl.multiple_of(head * DH, DH), DH)
        gate_feat = mix_taps(stream_gate, halo, taps, 0, cols)
        gate_send[cols, :] = gate_feat.astype(F32).T.astype(BF16)
        return unused

    lax.fori_loop(0, 8, gate_columns, 0)
    scatter(gate_send, gate_recv, 2)

    def query_out(step, unused):
        goal = lax.rem(pair + step, 32)
        remote(
            queries.at[
                pl.ds(pl.multiple_of(goal // 8 * 32, 32), 32),
                pl.ds(pl.multiple_of(goal % 8 * DH, DH), DH),
            ],
            query_all.at[query_rows, :],
            send_sem.at[5],
            recv_sem.at[5],
            goal * 2 + core,
        ).start()
        return unused

    lax.fori_loop(1, 32, query_out, 0)

    for load in loads[5:]:
        load.wait()
    wait_bytes(key_all.at[pl.ds(0, 7 * 128), :], recv_sem.at[4])
    keys_here = pl.ds(pl.multiple_of(across * 1024, 1024), 1024)

    def key_on(step, unused):
        remote(
            key_all.at[keys_here, :],
            key_all.at[keys_here, :],
            send_sem.at[6],
            recv_sem.at[6],
            lax.rem(across + step, 4) * 16 + depth * 2 + core,
        ).start()
        return unused

    lax.fori_loop(1, 4, key_on, 0)

    head_row = skip_gain[pl.ds(depth, 1), :]
    column[...] = jnp.broadcast_to(head_row, (DH, DH)).T
    skip_tile = column[rows16(my_block % 8), :]
    bias[...] = visible_bias(core, across)

    wait_bytes(filt_recv.at[rest, :], recv_sem.at[0])
    spectrum(filt_recv, wide, half, spec_h, outer_in, turns, inner_in)
    wait_bytes(prod_recv.at[rest, :], recv_sem.at[1])

    spectrum(prod_recv, wide, half, spec_x, outer_in, turns, inner_in)
    multiply_back(spec_x, spec_h, half, wide, turns, inner_out, outer_out)
    wait_bytes(gate_recv.at[rest, :], recv_sem.at[2])

    def gated(slot, unused):
        at = rows16(slot)
        inner = wide[at, :] + skip_tile * prod_recv[at, :].astype(F32)
        lanes = pl.ds(pl.multiple_of(slot * TOK, TOK), TOK)
        hyena[:, lanes] = (gate_recv[at, :].astype(F32) * inner).astype(BF16)
        return unused

    for chunk in range(4):
        lax.fori_loop(chunk * 8, chunk * 8 + 8, gated, 0, unroll=True)
        lax.fori_loop(32 + chunk * 8, 32 + chunk * 8 + 8, gated, 0, unroll=True)

        def value_out(step, unused):
            goal = lax.rem(member + step, 8)
            lanes = pl.ds(pl.multiple_of(goal % 2 * 4096 + chunk * 1024, 1024), 1024)
            remote(
                hyena.at[:, lanes],
                value_all.at[rows16(member), pl.ds(chunk * 1024, 1024)],
                value_out_sem.at[chunk],
                value_in_sem.at[chunk],
                goal // 2 * 16 + depth * 2 + goal % 2,
            ).start()
            return unused

        lax.fori_loop(1, 8, value_out, 0)
        lanes = pl.ds(pl.multiple_of(core * 4096 + chunk * 1024, 1024), 1024)
        value_all[rows16(member), pl.ds(chunk * 1024, 1024)] = hyena[:, lanes]

    def go_home(step, unused):
        dev = lax.rem(me + step, NC)
        remote(
            hyena.at[:, pl.ds(pl.multiple_of(slot_of(dev) * TOK, TOK), TOK)],
            home.at[rows16(my_block), :],
            send_sem.at[3],
            recv_sem.at[3],
            dev,
        ).start()
        return unused

    lax.fori_loop(1, NC, go_home, 0)
    home[rows16(my_block), :] = hyena[:, pl.ds(pl.multiple_of(my_slot * TOK, TOK), TOK)]

    wait_bytes(query_all.at[pl.ds(0, 31 * 32), :], recv_sem.at[5])
    queries_here = pl.ds(pl.multiple_of(core * 1024, 1024), 1024)
    query_on = remote(
        query_all.at[queries_here, :],
        query_all.at[queries_here, :],
        send_sem.at[7],
        recv_sem.at[7],
        sibling,
    )
    query_on.start()
    wait_bytes(key_all.at[pl.ds(0, 3 * 1024), :], recv_sem.at[6])
    query_on.wait_recv()

    attend_scores(core, query_all, key_all, (scores_even, scores_odd), bias, weights, stats)
    stats_out = remote(stats, other_stats, send_sem.at[9], recv_sem.at[9], sibling)
    stats_out.start()

    stats_out.wait_recv()

    def part_copy(block):
        return remote(
            part_send.at[block],
            part_recv.at[block],
            part_out.at[block],
            part_in.at[block],
            sibling,
        )

    def share(block):
        total = totals[block] * share_factor(block, stats, other_stats)
        own_part[block] = total[:, :128]
        part_send[block] = total[:, 128:].astype(BF16)
        part_copy(block).start()

    def settle(block):
        part_copy(block).wait_recv()
        whole = (own_part[block] + part_recv[block].astype(F32)).astype(BF16).astype(F32)
        att_send[pl.ds(block * 128, 128), :] = whole.T.astype(BF16)
        sum_own[block : block + 1, :] = (whole * whole).sum(axis=0, keepdims=True)

        for step in range(4):
            goal = block * 4 + lax.rem(depth + step, 4)
            rows = pl.ds(pl.multiple_of(goal * 32, 32), 32)

            @pl.when(goal != pair)
            def _():
                remote(
                    att_send.at[rows, :],
                    att_home.at[across_rows, my_cols],
                    send_sem.at[10],
                    recv_sem.at[10],
                    goal * 2 + core,
                ).start()

            @pl.when(goal == pair)
            def _():
                att_home[across_rows, my_cols] = att_send[rows, :]

    for chunk in range(4):
        wait_bytes(
            value_all.at[pl.ds(0, 7 * PIECE), pl.ds(chunk * 1024, 1024)], value_in_sem.at[chunk]
        )
        value_chunk(chunk, value_all, weights, totals)
        share(2 * chunk)
        share(2 * chunk + 1)
        if chunk > 0:
            settle(2 * chunk - 2)
            settle(2 * chunk - 1)
    settle(6)
    settle(7)

    sum_tp[tp] = sum_own[...]
    for step in range(1, 4):
        remote_tp(
            sum_own,
            sum_tp.at[tp],
            send_sem.at[11],
            recv_sem.at[11],
            lax.rem(tp + step, 4),
        ).start()
    wait_bytes(sum_tp.at[pl.ds(0, 3)], recv_sem.at[11])
    sum_send[...] = sum_tp[0] + sum_tp[1] + sum_tp[2] + sum_tp[3]

    def sums_out(step, unused):
        goal = lax.rem(pair + step, 32)
        remote(
            sum_send.at[pl.ds(goal // 4, 1), :],
            sum_home.at[pl.ds(pair, 1), :],
            send_sem.at[8],
            recv_sem.at[8],
            goal * 2 + core,
        ).start()
        return unused

    lax.fori_loop(1, 32, sums_out, 0)
    sum_home[pl.ds(pair, 1), :] = sum_send[pl.ds(pair // 4, 1), :]

    wait_bytes(home.at[rest, :], recv_sem.at[3])

    def finish(head, unused):
        cols = pl.ds(pl.multiple_of(head * DH, DH), DH)
        hyena_out[:, cols] = home[cols, :].astype(F32).T.astype(BF16)
        return unused

    lax.fori_loop(0, 8, finish, 0)

    wait_bytes(sum_home.at[pl.ds(0, 31), :], recv_sem.at[8])
    lane = lax.broadcasted_iota(jnp.int32, (1, TOK), 1)
    mean = jnp.zeros((1, TOK), F32)
    for group in range(4):
        part = sum_home[8 * group : 8 * group + 8, :].sum(axis=0, keepdims=True)
        part = pltpu.roll(jnp.broadcast_to(part, (8, TOK)), (group + 4 - pair % 4) * 32 % TOK, 1)
        mean = jnp.where(lane // 32 == group, part[0:1, :], mean)
    mean = mean * (1.0 / HC)
    inverse = jnp.broadcast_to(lax.rsqrt(mean + 1e-05), (TOK, TOK)).T
    wait_bytes(att_send.at[pl.ds(0, 31 * 32), :], recv_sem.at[10])
    for head in range(8):
        cols = slice(head * DH, (head + 1) * DH)
        part = att_home[:, cols].astype(F32)
        attn_out[:, cols] = (part * inverse * out_gain[0:1, cols]).astype(BF16)

    for index, send in enumerate((filt_send, prod_send, gate_send, home)):
        wait_bytes(send.at[rest, :], send_sem.at[index])
    wait_bytes(key_all.at[pl.ds(0, 7 * 128), :], send_sem.at[4])
    wait_bytes(query_all.at[pl.ds(0, 31 * 32), :], send_sem.at[5])
    wait_bytes(key_all.at[pl.ds(0, 3 * 1024), :], send_sem.at[6])
    query_on.wait_send()
    for chunk in range(4):
        wait_bytes(
            value_all.at[pl.ds(0, 7 * PIECE), pl.ds(chunk * 1024, 1024)], value_out_sem.at[chunk]
        )
    stats_out.wait_send()
    for block in range(8):
        part_copy(block).wait_send()
    wait_bytes(att_send.at[pl.ds(0, 31 * 32), :], send_sem.at[10])
    wait_bytes(sum_tp.at[pl.ds(0, 3)], send_sem.at[11])
    wait_bytes(sum_home.at[pl.ds(0, 31), :], send_sem.at[8])

    @pl.when(me < NC - 1)
    def _():
        for which, stream in enumerate(streams):
            wait_bytes(stream.at[pl.ds(TOK - 16, 16), :], halo_send.at[which])


def shards(
    queries, key_vectors, stream_gate, stream_key, stream_value,
    short_filter, long_filter, skip_gain, out_gain,
):
    vmem = pl.BlockSpec(memory_space=pltpu.VMEM)
    flat = pltpu.VMEM((NC * PIECE, TOK), BF16)
    dma = pltpu.SemaphoreType.DMA
    constants = dft_constants()
    shape = jax.ShapeDtypeStruct(stream_gate.shape, BF16)
    return pl.pallas_call(
        kernel,
        out_shape=(shape, shape),
        in_specs=[pl.BlockSpec(memory_space=pltpu.HBM)] * 14,
        out_specs=(vmem, vmem),
        scratch_shapes=[
            *[pltpu.VMEM((TOK, 1024), BF16)] * 3,
            pltpu.VMEM((3, 3, 1024), F32),
            pltpu.VMEM((1024, TOK), F32),
            pltpu.VMEM((8, DH), F32),
            pltpu.VMEM((1, 1024), F32),
            *[pltpu.VMEM(c.shape, c.dtype) for c in constants],
            pltpu.VMEM((3, 16, 1024), BF16),
            flat, flat, flat, flat, flat, flat,
            pltpu.VMEM((PIECE, NC * TOK), BF16),
            flat,
            pltpu.VMEM((NC * PIECE, TOK), F32),
            pltpu.VMEM((NC * PIECE, 2 * TOK), BF16),
            pltpu.VMEM((NC * PIECE, 2 * TOK), F32),
            pltpu.VMEM((NC * PIECE, 2 * TOK), F32),
            pltpu.VMEM((DH, DH), F32),
            pltpu.VMEM((2048, DH), BF16),
            pltpu.VMEM((4096, DH), BF16),
            pltpu.VMEM((DH, 4096), BF16),
            pltpu.VMEM((4096, QB), F32),
            pltpu.VMEM((4096, QB), F32),
            pltpu.VMEM((SPAN, QB), F32),
            pltpu.VMEM((36 * SPAN, QB), BF16),
            pltpu.VMEM((16, QB), F32),
            pltpu.VMEM((16, QB), F32),
            pltpu.VMEM((8, DH, QB), F32),
            pltpu.VMEM((8, DH, 128), F32),
            pltpu.VMEM((8, DH, 128), BF16),
            pltpu.VMEM((8, DH, 128), BF16),
            flat,
            pltpu.VMEM((TOK, 1024), BF16),
            pltpu.VMEM((8, TOK), F32),
            pltpu.VMEM((4, 8, TOK), F32),
            pltpu.VMEM((8, TOK), F32),
            pltpu.VMEM((32, TOK), F32),
            dma((12,)), dma((12,)), dma((3,)), dma((3,)), dma((8,)), dma((8,)),
            dma((14,)), dma((4,)), dma((4,)),
        ],
        compiler_params=pltpu.CompilerParams(
            collective_id=0, has_side_effects=True, vmem_limit_bytes=63 * 2**20
        ),
    )(
        queries, key_vectors, stream_gate, stream_key, stream_value, short_filter, long_filter,
        skip_gain.reshape(8, DH), out_gain.reshape(1, 1024), *constants,
    )


def solution(mesh):
    in_specs = (
        P("ctx", "tp"),
        P("ctx", "tp"),
        P("ctx", "tp"),
        P("ctx", "tp"),
        P("ctx", "tp"),
        P(None, None, "tp"),
        P("tp", "ctx"),
        P("tp"),
        P("tp"),
    )
    out_specs = (P("ctx", "tp"), P("ctx", "tp"))
    return jax.shard_map(shards, mesh=mesh, in_specs=in_specs, out_specs=out_specs, check_vma=False)
```

```python
import math

import jax
import jax.numpy as jnp
import numpy as np
from jax import lax
from jax.experimental import pallas as pl
from jax.experimental.pallas import tpu as pltpu
from jax.sharding import PartitionSpec as P

DH = 128
HC = 4096
NC = 64
TOK = 128
PIECE = 16
F32 = jnp.float32
BF16 = jnp.bfloat16
SPAN = 512
QB = 256
LOW = -1e30
SCALE = math.log2(math.e) / math.sqrt(DH)


def block_of(dev):
    return (dev // 2) % 8 * 8 + dev // 16 * 2 + dev % 2


def slot_of(dev):
    return dev % 2 * 32 + dev // 2


def dft_constants():
    slots = np.arange(NC)
    first = (2 * (slots % 32) + slots // 32).astype(np.float64)
    freq = np.arange(NC) + 0.25
    inner = np.arange(TOK)
    outer = 2 * np.pi * freq[:, None] * first[None, :] / NC
    turn = 2 * np.pi * freq[:, None] * inner[None, :] / (NC * TOK)
    mix = 2 * np.pi * (inner[:, None] * inner[None, :] % TOK) / TOK
    cos, sin = np.cos(mix), np.sin(mix)
    outer_in = np.concatenate([np.cos(outer), np.sin(outer)], axis=0)
    outer_out = np.concatenate([np.cos(outer), np.sin(outer)], axis=0).T / (NC * TOK)
    inner_in = np.block([[cos, sin], [-sin, cos]])
    inner_out = np.block([[cos, -sin], [sin, cos]])
    turns = np.stack([np.cos(turn), np.sin(turn)])
    return (
        jnp.asarray(outer_in, BF16),
        jnp.asarray(turns, F32),
        jnp.asarray(inner_in, BF16),
        jnp.asarray(inner_out, BF16),
        jnp.asarray(outer_out, BF16),
    )


def rows16(index):
    return pl.ds(pl.multiple_of(index * PIECE, PIECE), PIECE)


def remote(src, dst, send_sem, recv_sem, dev):
    return pltpu.make_async_remote_copy(
        src_ref=src,
        dst_ref=dst,
        send_sem=send_sem,
        recv_sem=recv_sem,
        device_id={"ctx": dev},
        device_id_type=pl.DeviceIdType.MESH,
    )


def wait_bytes(ref, sem):
    pltpu.make_async_copy(ref, ref, sem).wait()


def mix_taps(stream, halo, taps, which, cols):
    values = stream[:, cols].astype(F32)
    behind = halo[which, :, cols].astype(F32)
    row = lax.broadcasted_iota(jnp.int32, values.shape, 0)
    once = jnp.where(row == 0, behind[15:16], pltpu.roll(values, 1, 0))
    twice = pltpu.roll(values, 2, 0)
    twice = jnp.where(row == 0, behind[14:15], jnp.where(row == 1, behind[15:16], twice))
    mixed = (
        taps[which, 0:1, cols] * values
        + taps[which, 1:2, cols] * once
        + taps[which, 2:3, cols] * twice
    )
    return mixed.astype(BF16)


def spectrum(recv, wide, half, spec, outer_in, turns, inner_in):
    wide[...] = recv[...].astype(F32)
    turn_re, turn_im = turns[0], turns[1]
    for chan in range(0, PIECE, 2):
        pair = [wide[pl.ds(chan + k, NC, stride=PIECE), :].astype(BF16) for k in range(2)]
        both = jnp.dot(outer_in[...], jnp.concatenate(pair, axis=1), preferred_element_type=F32)
        for k in range(2):
            re, im = both[:NC, k * TOK : (k + 1) * TOK], both[NC:, k * TOK : (k + 1) * TOK]
            at = pl.ds((chan + k) * NC, NC)
            half[at, 0:TOK] = (re * turn_re - im * turn_im).astype(BF16)
            half[at, TOK : 2 * TOK] = (re * turn_im + im * turn_re).astype(BF16)
    for part in range(4):
        at = pl.ds(part * 256, 256)
        spec[at, :] = jnp.dot(half[at, :], inner_in[...], preferred_element_type=F32)


def multiply_back(spec_x, spec_h, half, wide, turns, inner_out, outer_out):
    turn_re, turn_im = turns[0], turns[1]
    for part in range(4):
        at = pl.ds(part * 256, 256)
        xr, xi = spec_x[at, 0:TOK], spec_x[at, TOK : 2 * TOK]
        hr, hi = spec_h[at, 0:TOK], spec_h[at, TOK : 2 * TOK]
        half[at, 0:TOK] = (xr * hr - xi * hi).astype(BF16)
        half[at, TOK : 2 * TOK] = (xr * hi + xi * hr).astype(BF16)
    for chan in range(0, PIECE, 2):
        back = jnp.dot(
            half[pl.ds(chan * NC, 2 * NC), :], inner_out[...], preferred_element_type=F32
        )
        pair = []
        for k in range(2):
            re, im = back[k * NC : (k + 1) * NC, :TOK], back[k * NC : (k + 1) * NC, TOK:]
            turned = jnp.concatenate(
                [re * turn_re + im * turn_im, im * turn_re - re * turn_im], axis=0
            )
            pair.append(turned.astype(BF16))
        both = jnp.dot(outer_out[...], jnp.concatenate(pair, axis=1), preferred_element_type=F32)
        for k in range(2):
            wide[pl.ds(chan + k, NC, stride=PIECE), :] = both[:, k * TOK : (k + 1) * TOK]


def span(chunk):
    return pl.ds(pl.multiple_of(chunk * SPAN, SPAN), SPAN)


def visible_bias(core, across):
    row = lax.broadcasted_iota(jnp.int32, (SPAN, QB), 0)
    lane = lax.broadcasted_iota(jnp.int32, (SPAN, QB), 1)
    key_pos = row // 128 * 256 + core * 128 + row % 128
    parity = jnp.where(lane < 128, core, 1 - core)
    query_pos = lane % 128 // 32 * 256 + parity * 128 + across * 32 + lane % 32
    return jnp.where(key_pos <= query_pos, 0.0, LOW)


def attend_scores(core, queries, keys, score_slots, bias, weights, stats):
    def both_halves(block):
        own = queries[pl.ds(pl.multiple_of(core * 1024 + block * 128, 128), 128), :]
        other = queries[pl.ds(pl.multiple_of((1 - core) * 1024 + block * 128, 128), 128), :]
        return jnp.concatenate([own, other], axis=0)

    def score(block, chunk, run_max, masked):
        here = lax.dot_general(
            keys[span(chunk), :],
            both_halves(block),
            (((1,), (1,)), ((), ())),
            preferred_element_type=F32,
        )
        if masked:
            here = here + bias[...]
        score_slots[block % 2][span(chunk), :] = here
        return jnp.maximum(run_max, here.reshape(SPAN // 8, 8, QB).max(axis=0))

    def weigh(block, chunk, top, total):
        terms = jnp.exp2(score_slots[block % 2][span(chunk), :] * SCALE - top)
        weights[span(block * (block + 1) // 2 + chunk), :] = terms.astype(BF16)
        return total + terms.reshape(SPAN // 8, 8, QB).sum(axis=0)

    lowest = jnp.full((8, QB), LOW, F32)
    none = jnp.zeros((8, QB), F32)
    run_max = lax.fori_loop(0, 7, lambda chunk, run: score(7, chunk, run, False), lowest, unroll=7)
    run_max = score(7, 7, run_max, True)
    for block in range(7, -1, -1):
        top = run_max.max(axis=0, keepdims=True) * SCALE

        def beside(chunk, carry, block=block, top=top):
            total, run = carry
            return (weigh(block, chunk, top, total), score(block - 1, chunk, run, False))

        total, run_max = lax.fori_loop(0, block - 1, beside, (none, lowest), unroll=2)
        if block > 0:
            total = weigh(block, block - 1, top, total)
            run_max = score(block - 1, block - 1, run_max, True)
        total = weigh(block, block, top, total)
        stats[block : block + 1, :] = top
        stats[8 + block : 9 + block, :] = total.sum(axis=0, keepdims=True)


def value_chunk(chunk, values, weights, totals):
    lanes = slice(chunk * 1024, (chunk + 1) * 1024)
    for block in range(2 * chunk, 8):
        first = (block * (block + 1) // 2 + 2 * chunk) * SPAN
        reach = SPAN if block == 2 * chunk else 2 * SPAN
        add = jnp.dot(
            values[:, lanes][:, :reach],
            weights[first : first + reach, :],
            preferred_element_type=F32,
        )
        totals[block] = add if chunk == 0 else totals[block] + add


def share_factor(block, stats, other_stats):
    top, count = stats[pl.ds(block, 1), :], stats[pl.ds(8 + block, 1), :]
    swap = lambda v: jnp.concatenate([v[:, 128:], v[:, :128]], axis=1)
    other_top = swap(other_stats[pl.ds(block, 1), :])
    other_count = swap(other_stats[pl.ds(8 + block, 1), :])
    both_top = jnp.maximum(top, other_top)
    mine = jnp.exp2(top - both_top)
    whole = mine * count + jnp.exp2(other_top - both_top) * other_count
    return mine / whole


def kernel(
    queries, key_vectors, gate_hbm, key_hbm, value_hbm,
    taps_hbm, filter_hbm, skip_hbm, gain_hbm,
    outer_in_hbm, turns_hbm, inner_in_hbm, inner_out_hbm, outer_out_hbm,
    hyena_out, attn_out,
    stream_gate, stream_key, stream_value, taps, long_filter, skip_gain, out_gain,
    outer_in, turns, inner_in, inner_out, outer_out,
    halo, filt_send, prod_send, gate_send, filt_recv, prod_recv, gate_recv,
    hyena, home, wide, half, spec_x, spec_h, column,
    query_all, key_all, value_all, scores_even, scores_odd, bias, weights, stats, other_stats,
    totals, own_part, part_send, part_recv, att_send, att_home, sum_own, sum_home,
    send_sem, recv_sem, halo_send, halo_recv, part_out, part_in,
    load_sem, value_out_sem, value_in_sem, plane_ready,
):
    me = lax.axis_index("ctx")
    tp = lax.axis_index("tp")
    across, depth, core = me // 16, (me // 2) % 8, me % 2
    pair, sibling = me // 2, me + 1 - 2 * core
    member = across * 2 + core
    my_block, my_slot = block_of(me), slot_of(me)
    barrier = pltpu.get_barrier_semaphore()

    def greet(step, unused):
        pl.semaphore_signal(
            barrier,
            inc=1,
            device_id={"ctx": lax.rem(me + step, NC)},
            device_id_type=pl.DeviceIdType.MESH,
        )
        return unused

    lax.fori_loop(1, NC, greet, 0)
    for step in range(1, 4):
        pl.semaphore_signal(
            barrier,
            inc=1,
            device_id={"tp": lax.rem(tp + step, 4)},
            device_id_type=pl.DeviceIdType.MESH,
        )
    loads = [
        pltpu.make_async_copy(src, dst, load_sem.at[index])
        for index, (src, dst) in enumerate(
            (
                (filter_hbm, long_filter),
                (taps_hbm, taps),
                (key_hbm, stream_key),
                (value_hbm, stream_value),
                (gate_hbm, stream_gate),
                (outer_in_hbm, outer_in),
                (turns_hbm, turns),
                (inner_in_hbm, inner_in),
                (inner_out_hbm, inner_out),
                (outer_out_hbm, outer_out),
                (skip_hbm, skip_gain),
                (gain_hbm, out_gain),
            )
        )
    ]
    key_rows = pl.ds(pl.multiple_of(pair * 128, 128), 128)
    query_rows = pl.ds(pl.multiple_of(core * 1024 + pair * 32, 32), 32)
    across_rows = pl.ds(pl.multiple_of(across * 32, 32), 32)
    my_cols = pl.ds(pl.multiple_of(depth * DH, DH), DH)
    loads.append(
        pltpu.make_async_copy(key_vectors.at[:, my_cols], key_all.at[key_rows, :], load_sem.at[12])
    )
    loads.append(
        pltpu.make_async_copy(
            queries.at[across_rows, my_cols], query_all.at[query_rows, :], load_sem.at[13]
        )
    )
    for load in loads:
        load.start()

    @pl.when(me == 0)
    def _():
        halo[...] = jnp.zeros_like(halo)

    loads[0].wait()
    filt_send[...] = long_filter[...].astype(BF16)
    pl.semaphore_wait(barrier, NC - 1 + 3)
    for step in range(1, 4):
        pl.semaphore_signal(
            plane_ready,
            inc=1,
            device_id={"tp": lax.rem(tp + step, 4)},
            device_id_type=pl.DeviceIdType.MESH,
        )

    streams = (gate_hbm, key_hbm, value_hbm)

    @pl.when(me < NC - 1)
    def _():
        for which, stream in enumerate(streams):
            remote(
                stream.at[pl.ds(TOK - 16, 16), :],
                halo.at[which],
                halo_send.at[which],
                halo_recv.at[which],
                me + 1,
            ).start()

    def key_out(step, unused):
        head = lax.rem(depth + step, 8)
        remote(
            key_vectors.at[:, pl.ds(pl.multiple_of(head * DH, DH), DH)],
            key_all.at[key_rows, :],
            send_sem.at[4],
            recv_sem.at[4],
            across * 16 + head * 2 + core,
        ).start()
        return unused

    lax.fori_loop(1, 8, key_out, 0)

    def scatter(send, recv, index):
        def one(step, unused):
            dev = lax.rem(me + step, NC)
            remote(
                send.at[rows16(block_of(dev)), :],
                recv.at[rows16(my_slot), :],
                send_sem.at[index],
                recv_sem.at[index],
                dev,
            ).start()
            return unused

        lax.fori_loop(1, NC, one, 0)
        recv[rows16(my_slot), :] = send[rows16(my_block), :]

    rest = pl.ds(0, (NC - 1) * PIECE)
    scatter(filt_send, filt_recv, 0)

    for load in loads[1:5]:
        load.wait()

    @pl.when(me > 0)
    def _():
        for which in range(3):
            wait_bytes(halo.at[which], halo_recv.at[which])

    def columns(head, unused):
        cols = pl.ds(pl.multiple_of(head * DH, DH), DH)
        key_feat = mix_taps(stream_key, halo, taps, 1, cols)
        value_feat = mix_taps(stream_value, halo, taps, 2, cols)
        product = key_feat.astype(F32) * value_feat.astype(F32)
        prod_send[cols, :] = product.T.astype(BF16)
        return unused

    lax.fori_loop(0, 8, columns, 0)
    scatter(prod_send, prod_recv, 1)

    def gate_columns(head, unused):
        cols = pl.ds(pl.multiple_of(head * DH, DH), DH)
        gate_feat = mix_taps(stream_gate, halo, taps, 0, cols)
        gate_send[cols, :] = gate_feat.astype(F32).T.astype(BF16)
        return unused

    lax.fori_loop(0, 8, gate_columns, 0)
    scatter(gate_send, gate_recv, 2)

    def query_out(step, unused):
        goal = lax.rem(pair + step, 32)
        remote(
            queries.at[
                pl.ds(pl.multiple_of(goal // 8 * 32, 32), 32),
                pl.ds(pl.multiple_of(goal % 8 * DH, DH), DH),
            ],
            query_all.at[query_rows, :],
            send_sem.at[5],
            recv_sem.at[5],
            goal * 2 + core,
        ).start()
        return unused

    lax.fori_loop(1, 32, query_out, 0)

    for load in loads[5:]:
        load.wait()
    wait_bytes(key_all.at[pl.ds(0, 7 * 128), :], recv_sem.at[4])
    keys_here = pl.ds(pl.multiple_of(across * 1024, 1024), 1024)

    def key_on(step, unused):
        remote(
            key_all.at[keys_here, :],
            key_all.at[keys_here, :],
            send_sem.at[6],
            recv_sem.at[6],
            lax.rem(across + step, 4) * 16 + depth * 2 + core,
        ).start()
        return unused

    lax.fori_loop(1, 4, key_on, 0)

    head_row = skip_gain[pl.ds(depth, 1), :]
    column[...] = jnp.broadcast_to(head_row, (DH, DH)).T
    skip_tile = column[rows16(my_block % 8), :]
    bias[...] = visible_bias(core, across)

    wait_bytes(filt_recv.at[rest, :], recv_sem.at[0])
    spectrum(filt_recv, wide, half, spec_h, outer_in, turns, inner_in)
    wait_bytes(prod_recv.at[rest, :], recv_sem.at[1])

    spectrum(prod_recv, wide, half, spec_x, outer_in, turns, inner_in)
    multiply_back(spec_x, spec_h, half, wide, turns, inner_out, outer_out)
    wait_bytes(gate_recv.at[rest, :], recv_sem.at[2])

    def gated(slot, unused):
        at = rows16(slot)
        inner = wide[at, :] + skip_tile * prod_recv[at, :].astype(F32)
        lanes = pl.ds(pl.multiple_of(slot * TOK, TOK), TOK)
        hyena[:, lanes] = (gate_recv[at, :].astype(F32) * inner).astype(BF16)
        return unused

    for chunk in range(4):
        lax.fori_loop(chunk * 8, chunk * 8 + 8, gated, 0, unroll=True)
        lax.fori_loop(32 + chunk * 8, 32 + chunk * 8 + 8, gated, 0, unroll=True)

        def value_out(step, unused):
            goal = lax.rem(member + step, 8)
            lanes = pl.ds(pl.multiple_of(goal % 2 * 4096 + chunk * 1024, 1024), 1024)
            remote(
                hyena.at[:, lanes],
                value_all.at[rows16(member), pl.ds(chunk * 1024, 1024)],
                value_out_sem.at[chunk],
                value_in_sem.at[chunk],
                goal // 2 * 16 + depth * 2 + goal % 2,
            ).start()
            return unused

        lax.fori_loop(1, 8, value_out, 0)
        lanes = pl.ds(pl.multiple_of(core * 4096 + chunk * 1024, 1024), 1024)
        value_all[rows16(member), pl.ds(chunk * 1024, 1024)] = hyena[:, lanes]

    def go_home(step, unused):
        dev = lax.rem(me + step, NC)
        remote(
            hyena.at[:, pl.ds(pl.multiple_of(slot_of(dev) * TOK, TOK), TOK)],
            home.at[rows16(my_block), :],
            send_sem.at[3],
            recv_sem.at[3],
            dev,
        ).start()
        return unused

    lax.fori_loop(1, NC, go_home, 0)
    home[rows16(my_block), :] = hyena[:, pl.ds(pl.multiple_of(my_slot * TOK, TOK), TOK)]

    wait_bytes(query_all.at[pl.ds(0, 31 * 32), :], recv_sem.at[5])
    queries_here = pl.ds(pl.multiple_of(core * 1024, 1024), 1024)
    query_on = remote(
        query_all.at[queries_here, :],
        query_all.at[queries_here, :],
        send_sem.at[7],
        recv_sem.at[7],
        sibling,
    )
    query_on.start()
    wait_bytes(key_all.at[pl.ds(0, 3 * 1024), :], recv_sem.at[6])
    query_on.wait_recv()

    attend_scores(core, query_all, key_all, (scores_even, scores_odd), bias, weights, stats)
    stats_out = remote(stats, other_stats, send_sem.at[9], recv_sem.at[9], sibling)
    stats_out.start()

    stats_out.wait_recv()
    pl.semaphore_wait(plane_ready, 3)

    def part_copy(block):
        return remote(
            part_send.at[block],
            part_recv.at[block],
            part_out.at[block],
            part_in.at[block],
            sibling,
        )

    def share(block):
        total = totals[block] * share_factor(block, stats, other_stats)
        own_part[block] = total[:, :128]
        part_send[block] = total[:, 128:].astype(BF16)
        part_copy(block).start()

    def sum_copy(block, goal, row):
        return pltpu.make_async_remote_copy(
            src_ref=sum_own.at[pl.ds(block, 1), :],
            dst_ref=sum_home.at[pl.ds(tp * 32 + pair, 1), :],
            send_sem=send_sem.at[8],
            recv_sem=recv_sem.at[8],
            device_id={"ctx": goal * 2 + core, "tp": row},
            device_id_type=pl.DeviceIdType.MESH,
        )

    def settle(block):
        part_copy(block).wait_recv()
        whole = (own_part[block] + part_recv[block].astype(F32)).astype(BF16).astype(F32)
        att_send[pl.ds(block * 128, 128), :] = whole.T.astype(BF16)
        sum_own[block : block + 1, :] = (whole * whole).sum(axis=0, keepdims=True)

        def send(step, unused):
            goal = block * 4 + lax.rem(depth + step, 4)
            rows = pl.ds(pl.multiple_of(goal * 32, 32), 32)

            @pl.when(goal != pair)
            def _():
                remote(
                    att_send.at[rows, :],
                    att_home.at[across_rows, my_cols],
                    send_sem.at[10],
                    recv_sem.at[10],
                    goal * 2 + core,
                ).start()
                sum_copy(block, goal, tp).start()

            @pl.when(goal == pair)
            def _():
                att_home[across_rows, my_cols] = att_send[rows, :]
                sum_home[pl.ds(tp * 32 + pair, 1), :] = sum_own[pl.ds(block, 1), :]

            for other in range(1, 4):
                sum_copy(block, goal, lax.rem(tp + other, 4)).start()
            return unused

        lax.fori_loop(0, 4, send, 0)

    for chunk in range(4):
        wait_bytes(
            value_all.at[pl.ds(0, 7 * PIECE), pl.ds(chunk * 1024, 1024)], value_in_sem.at[chunk]
        )
        value_chunk(chunk, value_all, weights, totals)
        share(2 * chunk)
        share(2 * chunk + 1)
        settle(2 * chunk)
        settle(2 * chunk + 1)

    wait_bytes(home.at[rest, :], recv_sem.at[3])

    def finish(head, unused):
        cols = pl.ds(pl.multiple_of(head * DH, DH), DH)
        hyena_out[:, cols] = home[cols, :].astype(F32).T.astype(BF16)
        return unused

    lax.fori_loop(0, 8, finish, 0)

    wait_bytes(sum_home.at[pl.ds(0, 127), :], recv_sem.at[8])
    lane = lax.broadcasted_iota(jnp.int32, (1, TOK), 1)
    mean = jnp.zeros((1, TOK), F32)
    for group in range(4):
        part = sum_home[8 * group : 8 * group + 8, :]
        for row in range(1, 4):
            part = part + sum_home[32 * row + 8 * group : 32 * row + 8 * group + 8, :]
        part = jnp.broadcast_to(part.sum(axis=0, keepdims=True), (8, TOK))
        part = pltpu.roll(part, (group + 4 - pair % 4) * 32 % TOK, 1)
        mean = jnp.where(lane // 32 == group, part[0:1, :], mean)
    mean = mean * (1.0 / HC)
    inverse = jnp.broadcast_to(lax.rsqrt(mean + 1e-05), (TOK, TOK)).T
    wait_bytes(att_send.at[pl.ds(0, 31 * 32), :], recv_sem.at[10])
    for head in range(8):
        cols = slice(head * DH, (head + 1) * DH)
        part = att_home[:, cols].astype(F32)
        attn_out[:, cols] = (part * inverse * out_gain[0:1, cols]).astype(BF16)

    for index, send in enumerate((filt_send, prod_send, gate_send, home)):
        wait_bytes(send.at[rest, :], send_sem.at[index])
    wait_bytes(key_all.at[pl.ds(0, 7 * 128), :], send_sem.at[4])
    wait_bytes(query_all.at[pl.ds(0, 31 * 32), :], send_sem.at[5])
    wait_bytes(key_all.at[pl.ds(0, 3 * 1024), :], send_sem.at[6])
    query_on.wait_send()
    for chunk in range(4):
        wait_bytes(
            value_all.at[pl.ds(0, 7 * PIECE), pl.ds(chunk * 1024, 1024)], value_out_sem.at[chunk]
        )
    stats_out.wait_send()
    for block in range(8):
        part_copy(block).wait_send()
    wait_bytes(att_send.at[pl.ds(0, 31 * 32), :], send_sem.at[10])
    wait_bytes(sum_home.at[pl.ds(0, 127), :], send_sem.at[8])

    @pl.when(me < NC - 1)
    def _():
        for which, stream in enumerate(streams):
            wait_bytes(stream.at[pl.ds(TOK - 16, 16), :], halo_send.at[which])


def shards(
    queries, key_vectors, stream_gate, stream_key, stream_value,
    short_filter, long_filter, skip_gain, out_gain,
):
    vmem = pl.BlockSpec(memory_space=pltpu.VMEM)
    flat = pltpu.VMEM((NC * PIECE, TOK), BF16)
    dma = pltpu.SemaphoreType.DMA
    constants = dft_constants()
    shape = jax.ShapeDtypeStruct(stream_gate.shape, BF16)
    return pl.pallas_call(
        kernel,
        out_shape=(shape, shape),
        in_specs=[pl.BlockSpec(memory_space=pltpu.HBM)] * 14,
        out_specs=(vmem, vmem),
        scratch_shapes=[
            *[pltpu.VMEM((TOK, 1024), BF16)] * 3,
            pltpu.VMEM((3, 3, 1024), F32),
            pltpu.VMEM((1024, TOK), F32),
            pltpu.VMEM((8, DH), F32),
            pltpu.VMEM((1, 1024), F32),
            *[pltpu.VMEM(c.shape, c.dtype) for c in constants],
            pltpu.VMEM((3, 16, 1024), BF16),
            flat, flat, flat, flat, flat, flat,
            pltpu.VMEM((PIECE, NC * TOK), BF16),
            flat,
            pltpu.VMEM((NC * PIECE, TOK), F32),
            pltpu.VMEM((NC * PIECE, 2 * TOK), BF16),
            pltpu.VMEM((NC * PIECE, 2 * TOK), F32),
            pltpu.VMEM((NC * PIECE, 2 * TOK), F32),
            pltpu.VMEM((DH, DH), F32),
            pltpu.VMEM((2048, DH), BF16),
            pltpu.VMEM((4096, DH), BF16),
            pltpu.VMEM((DH, 4096), BF16),
            pltpu.VMEM((4096, QB), F32),
            pltpu.VMEM((4096, QB), F32),
            pltpu.VMEM((SPAN, QB), F32),
            pltpu.VMEM((36 * SPAN, QB), BF16),
            pltpu.VMEM((16, QB), F32),
            pltpu.VMEM((16, QB), F32),
            pltpu.VMEM((8, DH, QB), F32),
            pltpu.VMEM((8, DH, 128), F32),
            pltpu.VMEM((8, DH, 128), BF16),
            pltpu.VMEM((8, DH, 128), BF16),
            flat,
            pltpu.VMEM((TOK, 1024), BF16),
            pltpu.VMEM((8, TOK), F32),
            pltpu.VMEM((128, TOK), F32),
            dma((12,)), dma((12,)), dma((3,)), dma((3,)), dma((8,)), dma((8,)),
            dma((14,)), dma((4,)), dma((4,)), pltpu.SemaphoreType.REGULAR,
        ],
        compiler_params=pltpu.CompilerParams(
            collective_id=0, has_side_effects=True, vmem_limit_bytes=63 * 2**20
        ),
    )(
        queries, key_vectors, stream_gate, stream_key, stream_value, short_filter, long_filter,
        skip_gain.reshape(8, DH), out_gain.reshape(1, 1024), *constants,
    )


def solution(mesh):
    in_specs = (
        P("ctx", "tp"),
        P("ctx", "tp"),
        P("ctx", "tp"),
        P("ctx", "tp"),
        P("ctx", "tp"),
        P(None, None, "tp"),
        P("tp", "ctx"),
        P("tp"),
        P("tp"),
    )
    out_specs = (P("ctx", "tp"), P("ctx", "tp"))
    return jax.shard_map(shards, mesh=mesh, in_specs=in_specs, out_specs=out_specs, check_vma=False)
```

```python
import math

import jax
import jax.numpy as jnp
import numpy as np
from jax import lax
from jax.experimental import pallas as pl
from jax.experimental.pallas import tpu as pltpu
from jax.sharding import PartitionSpec as P

DH = 128
HC = 4096
NC = 64
TOK = 128
PIECE = 16
F32 = jnp.float32
BF16 = jnp.bfloat16
SPAN = 512
QB = 256
LOW = -1e30
SCALE = math.log2(math.e) / math.sqrt(DH)


def block_of(dev):
    return (dev // 2) % 8 * 8 + dev // 16 * 2 + dev % 2


def slot_of(dev):
    return dev % 2 * 32 + dev // 2


def dft_constants():
    slots = np.arange(NC)
    first = (2 * (slots % 32) + slots // 32).astype(np.float64)
    freq = np.arange(NC) + 0.25
    inner = np.arange(TOK)
    outer = 2 * np.pi * freq[:, None] * first[None, :] / NC
    turn = 2 * np.pi * freq[:, None] * inner[None, :] / (NC * TOK)
    mix = 2 * np.pi * (inner[:, None] * inner[None, :] % TOK) / TOK
    cos, sin = np.cos(mix), np.sin(mix)
    outer_in = np.concatenate([np.cos(outer), np.sin(outer)], axis=0)
    outer_out = np.concatenate([np.cos(outer), np.sin(outer)], axis=0).T / (NC * TOK)
    inner_in = np.block([[cos, sin], [-sin, cos]])
    inner_out = np.block([[cos, -sin], [sin, cos]])
    turns = np.stack([np.cos(turn), np.sin(turn)])
    return (
        jnp.asarray(outer_in, BF16),
        jnp.asarray(turns, F32),
        jnp.asarray(inner_in, BF16),
        jnp.asarray(inner_out, BF16),
        jnp.asarray(outer_out, BF16),
    )


def rows16(index):
    return pl.ds(pl.multiple_of(index * PIECE, PIECE), PIECE)


def remote(src, dst, send_sem, recv_sem, dev):
    return pltpu.make_async_remote_copy(
        src_ref=src,
        dst_ref=dst,
        send_sem=send_sem,
        recv_sem=recv_sem,
        device_id={"ctx": dev},
        device_id_type=pl.DeviceIdType.MESH,
    )


def wait_bytes(ref, sem):
    pltpu.make_async_copy(ref, ref, sem).wait()


def mix_taps(stream, halo, taps, which, cols):
    values = stream[:, cols].astype(F32)
    behind = halo[which, :, cols].astype(F32)
    row = lax.broadcasted_iota(jnp.int32, values.shape, 0)
    once = jnp.where(row == 0, behind[15:16], pltpu.roll(values, 1, 0))
    twice = pltpu.roll(values, 2, 0)
    twice = jnp.where(row == 0, behind[14:15], jnp.where(row == 1, behind[15:16], twice))
    mixed = (
        taps[which, 0:1, cols] * values
        + taps[which, 1:2, cols] * once
        + taps[which, 2:3, cols] * twice
    )
    return mixed.astype(BF16)


def spectrum(recv, wide, half, spec, outer_in, turns, inner_in):
    wide[...] = recv[...].astype(F32)
    turn_re, turn_im = turns[0], turns[1]
    for chan in range(0, PIECE, 2):
        pair = [wide[pl.ds(chan + k, NC, stride=PIECE), :].astype(BF16) for k in range(2)]
        both = jnp.dot(outer_in[...], jnp.concatenate(pair, axis=1), preferred_element_type=F32)
        for k in range(2):
            re, im = both[:NC, k * TOK : (k + 1) * TOK], both[NC:, k * TOK : (k + 1) * TOK]
            at = pl.ds((chan + k) * NC, NC)
            half[at, 0:TOK] = (re * turn_re - im * turn_im).astype(BF16)
            half[at, TOK : 2 * TOK] = (re * turn_im + im * turn_re).astype(BF16)
    for part in range(4):
        at = pl.ds(part * 256, 256)
        spec[at, :] = jnp.dot(half[at, :], inner_in[...], preferred_element_type=F32)


def multiply_back(spec_x, spec_h, half, wide, turns, inner_out, outer_out):
    turn_re, turn_im = turns[0], turns[1]
    for part in range(4):
        at = pl.ds(part * 256, 256)
        xr, xi = spec_x[at, 0:TOK], spec_x[at, TOK : 2 * TOK]
        hr, hi = spec_h[at, 0:TOK], spec_h[at, TOK : 2 * TOK]
        half[at, 0:TOK] = (xr * hr - xi * hi).astype(BF16)
        half[at, TOK : 2 * TOK] = (xr * hi + xi * hr).astype(BF16)
    for chan in range(0, PIECE, 2):
        back = jnp.dot(
            half[pl.ds(chan * NC, 2 * NC), :], inner_out[...], preferred_element_type=F32
        )
        pair = []
        for k in range(2):
            re, im = back[k * NC : (k + 1) * NC, :TOK], back[k * NC : (k + 1) * NC, TOK:]
            turned = jnp.concatenate(
                [re * turn_re + im * turn_im, im * turn_re - re * turn_im], axis=0
            )
            pair.append(turned.astype(BF16))
        both = jnp.dot(outer_out[...], jnp.concatenate(pair, axis=1), preferred_element_type=F32)
        for k in range(2):
            wide[pl.ds(chan + k, NC, stride=PIECE), :] = both[:, k * TOK : (k + 1) * TOK]


def span(chunk):
    return pl.ds(pl.multiple_of(chunk * SPAN, SPAN), SPAN)


def visible_bias(core, across):
    row = lax.broadcasted_iota(jnp.int32, (SPAN, QB), 0)
    lane = lax.broadcasted_iota(jnp.int32, (SPAN, QB), 1)
    key_pos = row // 128 * 256 + core * 128 + row % 128
    parity = jnp.where(lane < 128, core, 1 - core)
    query_pos = lane % 128 // 32 * 256 + parity * 128 + across * 32 + lane % 32
    return jnp.where(key_pos <= query_pos, 0.0, LOW)


def attend_scores(core, queries, keys, score_slots, bias, weights, stats):
    def both_halves(block):
        own = queries[pl.ds(pl.multiple_of(core * 1024 + block * 128, 128), 128), :]
        other = queries[pl.ds(pl.multiple_of((1 - core) * 1024 + block * 128, 128), 128), :]
        return jnp.concatenate([own, other], axis=0)

    def score(block, chunk, run_max, masked):
        here = lax.dot_general(
            keys[span(chunk), :],
            both_halves(block),
            (((1,), (1,)), ((), ())),
            preferred_element_type=F32,
        )
        if masked:
            here = here + bias[...]
        score_slots[block % 2][span(chunk), :] = here
        return jnp.maximum(run_max, here.reshape(SPAN // 8, 8, QB).max(axis=0))

    def weigh(block, chunk, top, total):
        terms = jnp.exp2(score_slots[block % 2][span(chunk), :] * SCALE - top)
        weights[span(block * (block + 1) // 2 + chunk), :] = terms.astype(BF16)
        return total + terms.reshape(SPAN // 8, 8, QB).sum(axis=0)

    lowest = jnp.full((8, QB), LOW, F32)
    none = jnp.zeros((8, QB), F32)
    run_max = lax.fori_loop(0, 7, lambda chunk, run: score(7, chunk, run, False), lowest, unroll=7)
    run_max = score(7, 7, run_max, True)
    for block in range(7, -1, -1):
        top = run_max.max(axis=0, keepdims=True) * SCALE

        def beside(chunk, carry, block=block, top=top):
            total, run = carry
            return (weigh(block, chunk, top, total), score(block - 1, chunk, run, False))

        total, run_max = lax.fori_loop(0, block - 1, beside, (none, lowest), unroll=2)
        if block > 0:
            total = weigh(block, block - 1, top, total)
            run_max = score(block - 1, block - 1, run_max, True)
        total = weigh(block, block, top, total)
        stats[block : block + 1, :] = top
        stats[8 + block : 9 + block, :] = total.sum(axis=0, keepdims=True)


def value_chunk(chunk, values, weights, totals):
    lanes = slice(chunk * 1024, (chunk + 1) * 1024)
    for block in range(2 * chunk, 8):
        first = (block * (block + 1) // 2 + 2 * chunk) * SPAN
        reach = SPAN if block == 2 * chunk else 2 * SPAN
        add = jnp.dot(
            values[:, lanes][:, :reach],
            weights[first : first + reach, :],
            preferred_element_type=F32,
        )
        totals[block] = add if chunk == 0 else totals[block] + add


def share_factor(block, stats, other_stats):
    top, count = stats[pl.ds(block, 1), :], stats[pl.ds(8 + block, 1), :]
    swap = lambda v: jnp.concatenate([v[:, 128:], v[:, :128]], axis=1)
    other_top = swap(other_stats[pl.ds(block, 1), :])
    other_count = swap(other_stats[pl.ds(8 + block, 1), :])
    both_top = jnp.maximum(top, other_top)
    mine = jnp.exp2(top - both_top)
    whole = mine * count + jnp.exp2(other_top - both_top) * other_count
    return mine / whole


def kernel(
    queries, key_vectors, gate_hbm, key_hbm, value_hbm,
    taps_hbm, filter_hbm, skip_hbm,
    outer_in_hbm, turns_hbm, inner_in_hbm, inner_out_hbm, outer_out_hbm,
    home_out, att_out, inverse_out,
    stream_gate, stream_key, stream_value, taps, long_filter, skip_gain,
    outer_in, turns, inner_in, inner_out, outer_out,
    halo, filt_send, prod_send, gate_send, filt_recv, prod_recv, gate_recv,
    hyena, home, wide, half, spec_x, spec_h, column,
    query_all, key_all, value_all, scores_even, scores_odd, bias, weights, stats, other_stats,
    totals, own_part, part_send, part_recv, att_send, att_home, sum_own, sum_home, inverse,
    send_sem, recv_sem, halo_send, halo_recv, part_out, part_in,
    load_sem, value_out_sem, value_in_sem, plane_ready,
):
    me = lax.axis_index("ctx")
    tp = lax.axis_index("tp")
    across, depth, core = me // 16, (me // 2) % 8, me % 2
    pair, sibling = me // 2, me + 1 - 2 * core
    member = across * 2 + core
    my_block, my_slot = block_of(me), slot_of(me)
    barrier = pltpu.get_barrier_semaphore()

    def greet(step, unused):
        pl.semaphore_signal(
            barrier,
            inc=1,
            device_id={"ctx": lax.rem(me + step, NC)},
            device_id_type=pl.DeviceIdType.MESH,
        )
        return unused

    lax.fori_loop(1, NC, greet, 0)
    for step in range(1, 4):
        pl.semaphore_signal(
            barrier,
            inc=1,
            device_id={"tp": lax.rem(tp + step, 4)},
            device_id_type=pl.DeviceIdType.MESH,
        )
    loads = [
        pltpu.make_async_copy(src, dst, load_sem.at[index])
        for index, (src, dst) in enumerate(
            (
                (filter_hbm, long_filter),
                (taps_hbm, taps),
                (key_hbm, stream_key),
                (value_hbm, stream_value),
                (gate_hbm, stream_gate),
                (outer_in_hbm, outer_in),
                (turns_hbm, turns),
                (inner_in_hbm, inner_in),
                (inner_out_hbm, inner_out),
                (outer_out_hbm, outer_out),
                (skip_hbm, skip_gain),
            )
        )
    ]
    key_rows = pl.ds(pl.multiple_of(pair * 128, 128), 128)
    query_rows = pl.ds(pl.multiple_of(core * 1024 + pair * 32, 32), 32)
    across_rows = pl.ds(pl.multiple_of(across * 32, 32), 32)
    my_cols = pl.ds(pl.multiple_of(depth * DH, DH), DH)
    loads.append(
        pltpu.make_async_copy(key_vectors.at[:, my_cols], key_all.at[key_rows, :], load_sem.at[12])
    )
    loads.append(
        pltpu.make_async_copy(
            queries.at[across_rows, my_cols], query_all.at[query_rows, :], load_sem.at[13]
        )
    )
    for load in loads:
        load.start()

    @pl.when(me == 0)
    def _():
        halo[...] = jnp.zeros_like(halo)

    loads[0].wait()
    filt_send[...] = long_filter[...].astype(BF16)
    pl.semaphore_wait(barrier, NC - 1 + 3)
    for step in range(1, 4):
        pl.semaphore_signal(
            plane_ready,
            inc=1,
            device_id={"tp": lax.rem(tp + step, 4)},
            device_id_type=pl.DeviceIdType.MESH,
        )

    streams = (gate_hbm, key_hbm, value_hbm)

    @pl.when(me < NC - 1)
    def _():
        for which, stream in enumerate(streams):
            remote(
                stream.at[pl.ds(TOK - 16, 16), :],
                halo.at[which],
                halo_send.at[which],
                halo_recv.at[which],
                me + 1,
            ).start()

    def key_out(step, unused):
        head = lax.rem(depth + step, 8)
        remote(
            key_vectors.at[:, pl.ds(pl.multiple_of(head * DH, DH), DH)],
            key_all.at[key_rows, :],
            send_sem.at[4],
            recv_sem.at[4],
            across * 16 + head * 2 + core,
        ).start()
        return unused

    lax.fori_loop(1, 8, key_out, 0)

    def scatter(send, recv, index):
        def one(step, unused):
            dev = lax.rem(me + step, NC)
            remote(
                send.at[rows16(block_of(dev)), :],
                recv.at[rows16(my_slot), :],
                send_sem.at[index],
                recv_sem.at[index],
                dev,
            ).start()
            return unused

        lax.fori_loop(1, NC, one, 0)
        recv[rows16(my_slot), :] = send[rows16(my_block), :]

    rest = pl.ds(0, (NC - 1) * PIECE)
    scatter(filt_send, filt_recv, 0)

    for load in loads[1:5]:
        load.wait()

    @pl.when(me > 0)
    def _():
        for which in range(3):
            wait_bytes(halo.at[which], halo_recv.at[which])

    def columns(head, unused):
        cols = pl.ds(pl.multiple_of(head * DH, DH), DH)
        key_feat = mix_taps(stream_key, halo, taps, 1, cols)
        value_feat = mix_taps(stream_value, halo, taps, 2, cols)
        product = key_feat.astype(F32) * value_feat.astype(F32)
        prod_send[cols, :] = product.T.astype(BF16)
        return unused

    lax.fori_loop(0, 8, columns, 0, unroll=2)
    scatter(prod_send, prod_recv, 1)

    def gate_columns(head, unused):
        cols = pl.ds(pl.multiple_of(head * DH, DH), DH)
        gate_feat = mix_taps(stream_gate, halo, taps, 0, cols)
        gate_send[cols, :] = gate_feat.astype(F32).T.astype(BF16)
        return unused

    lax.fori_loop(0, 8, gate_columns, 0, unroll=2)
    scatter(gate_send, gate_recv, 2)

    def query_out(step, unused):
        goal = lax.rem(pair + step, 32)
        remote(
            queries.at[
                pl.ds(pl.multiple_of(goal // 8 * 32, 32), 32),
                pl.ds(pl.multiple_of(goal % 8 * DH, DH), DH),
            ],
            query_all.at[query_rows, :],
            send_sem.at[5],
            recv_sem.at[5],
            goal * 2 + core,
        ).start()
        return unused

    lax.fori_loop(1, 32, query_out, 0)

    for load in loads[5:]:
        load.wait()
    wait_bytes(key_all.at[pl.ds(0, 7 * 128), :], recv_sem.at[4])
    keys_here = pl.ds(pl.multiple_of(across * 1024, 1024), 1024)

    def key_on(step, unused):
        remote(
            key_all.at[keys_here, :],
            key_all.at[keys_here, :],
            send_sem.at[6],
            recv_sem.at[6],
            lax.rem(across + step, 4) * 16 + depth * 2 + core,
        ).start()
        return unused

    lax.fori_loop(1, 4, key_on, 0)

    head_row = skip_gain[pl.ds(depth, 1), :]
    column[...] = jnp.broadcast_to(head_row, (DH, DH)).T
    skip_tile = column[rows16(my_block % 8), :]
    bias[...] = visible_bias(core, across)

    wait_bytes(filt_recv.at[rest, :], recv_sem.at[0])
    spectrum(filt_recv, wide, half, spec_h, outer_in, turns, inner_in)
    wait_bytes(prod_recv.at[rest, :], recv_sem.at[1])

    spectrum(prod_recv, wide, half, spec_x, outer_in, turns, inner_in)
    multiply_back(spec_x, spec_h, half, wide, turns, inner_out, outer_out)
    wait_bytes(gate_recv.at[rest, :], recv_sem.at[2])

    def gated(slot, unused):
        at = rows16(slot)
        inner = wide[at, :] + skip_tile * prod_recv[at, :].astype(F32)
        lanes = pl.ds(pl.multiple_of(slot * TOK, TOK), TOK)
        hyena[:, lanes] = (gate_recv[at, :].astype(F32) * inner).astype(BF16)
        return unused

    for chunk in range(4):
        lax.fori_loop(chunk * 8, chunk * 8 + 8, gated, 0, unroll=True)
        lax.fori_loop(32 + chunk * 8, 32 + chunk * 8 + 8, gated, 0, unroll=True)

        def value_out(step, unused):
            goal = lax.rem(member + step, 8)
            lanes = pl.ds(pl.multiple_of(goal % 2 * 4096 + chunk * 1024, 1024), 1024)
            remote(
                hyena.at[:, lanes],
                value_all.at[rows16(member), pl.ds(chunk * 1024, 1024)],
                value_out_sem.at[chunk],
                value_in_sem.at[chunk],
                goal // 2 * 16 + depth * 2 + goal % 2,
            ).start()
            return unused

        lax.fori_loop(1, 8, value_out, 0)
        lanes = pl.ds(pl.multiple_of(core * 4096 + chunk * 1024, 1024), 1024)
        value_all[rows16(member), pl.ds(chunk * 1024, 1024)] = hyena[:, lanes]

    def go_home(step, unused):
        dev = lax.rem(me + step, NC)
        remote(
            hyena.at[:, pl.ds(pl.multiple_of(slot_of(dev) * TOK, TOK), TOK)],
            home.at[rows16(my_block), :],
            send_sem.at[3],
            recv_sem.at[3],
            dev,
        ).start()
        return unused

    lax.fori_loop(1, NC, go_home, 0, unroll=9)
    home[rows16(my_block), :] = hyena[:, pl.ds(pl.multiple_of(my_slot * TOK, TOK), TOK)]

    wait_bytes(query_all.at[pl.ds(0, 31 * 32), :], recv_sem.at[5])
    queries_here = pl.ds(pl.multiple_of(core * 1024, 1024), 1024)
    query_on = remote(
        query_all.at[queries_here, :],
        query_all.at[queries_here, :],
        send_sem.at[7],
        recv_sem.at[7],
        sibling,
    )
    query_on.start()
    wait_bytes(key_all.at[pl.ds(0, 3 * 1024), :], recv_sem.at[6])
    query_on.wait_recv()

    attend_scores(core, query_all, key_all, (scores_even, scores_odd), bias, weights, stats)
    stats_out = remote(stats, other_stats, send_sem.at[9], recv_sem.at[9], sibling)
    stats_out.start()

    stats_out.wait_recv()
    pl.semaphore_wait(plane_ready, 3)

    def part_copy(block):
        return remote(
            part_send.at[block],
            part_recv.at[block],
            part_out.at[block],
            part_in.at[block],
            sibling,
        )

    def share(block):
        total = totals[block] * share_factor(block, stats, other_stats)
        own_part[block] = total[:, :128]
        part_send[block] = total[:, 128:].astype(BF16)
        part_copy(block).start()

    def sum_copy(block, goal, row):
        return pltpu.make_async_remote_copy(
            src_ref=sum_own.at[pl.ds(block, 1), :],
            dst_ref=sum_home.at[pl.ds(tp * 32 + pair, 1), :],
            send_sem=send_sem.at[8],
            recv_sem=recv_sem.at[8],
            device_id={"ctx": goal * 2 + core, "tp": row},
            device_id_type=pl.DeviceIdType.MESH,
        )

    def settle(block):
        part_copy(block).wait_recv()
        whole = (own_part[block] + part_recv[block].astype(F32)).astype(BF16).astype(F32)
        att_send[pl.ds(block * 128, 128), :] = whole.T.astype(BF16)
        sum_own[block : block + 1, :] = (whole * whole).sum(axis=0, keepdims=True)

        def send(step, unused):
            goal = block * 4 + lax.rem(depth + step, 4)
            rows = pl.ds(pl.multiple_of(goal * 32, 32), 32)

            @pl.when(goal != pair)
            def _():
                remote(
                    att_send.at[rows, :],
                    att_home.at[across_rows, my_cols],
                    send_sem.at[10],
                    recv_sem.at[10],
                    goal * 2 + core,
                ).start()
                sum_copy(block, goal, tp).start()

            @pl.when(goal == pair)
            def _():
                att_home[across_rows, my_cols] = att_send[rows, :]
                sum_home[pl.ds(tp * 32 + pair, 1), :] = sum_own[pl.ds(block, 1), :]

            for other in range(1, 4):
                sum_copy(block, goal, lax.rem(tp + other, 4)).start()
            return unused

        lax.fori_loop(0, 4, send, 0, unroll=True)

    for chunk in range(4):
        wait_bytes(
            value_all.at[pl.ds(0, 7 * PIECE), pl.ds(chunk * 1024, 1024)], value_in_sem.at[chunk]
        )
        value_chunk(chunk, value_all, weights, totals)
        share(2 * chunk)
        share(2 * chunk + 1)
        settle(2 * chunk)
        settle(2 * chunk + 1)

    wait_bytes(home.at[rest, :], recv_sem.at[3])

    home_copy = pltpu.make_async_copy(home, home_out, load_sem.at[14])
    home_copy.start()

    wait_bytes(sum_home.at[pl.ds(0, 127), :], recv_sem.at[8])
    lane = lax.broadcasted_iota(jnp.int32, (1, TOK), 1)
    mean = jnp.zeros((1, TOK), F32)
    for group in range(4):
        part = sum_home[8 * group : 8 * group + 8, :]
        for row in range(1, 4):
            part = part + sum_home[32 * row + 8 * group : 32 * row + 8 * group + 8, :]
        part = jnp.broadcast_to(part.sum(axis=0, keepdims=True), (8, TOK))
        part = pltpu.roll(part, (group + 4 - pair % 4) * 32 % TOK, 1)
        mean = jnp.where(lane // 32 == group, part[0:1, :], mean)
    mean = mean * (1.0 / HC)
    inverse[...] = jnp.broadcast_to(lax.rsqrt(mean + 1e-05), (8, TOK))
    inverse_copy = pltpu.make_async_copy(inverse, inverse_out, load_sem.at[15])
    inverse_copy.start()
    wait_bytes(att_send.at[pl.ds(0, 31 * 32), :], recv_sem.at[10])
    att_copy = pltpu.make_async_copy(att_home, att_out, load_sem.at[16])
    att_copy.start()

    for index, send in enumerate((filt_send, prod_send, gate_send, home)):
        wait_bytes(send.at[rest, :], send_sem.at[index])
    wait_bytes(key_all.at[pl.ds(0, 7 * 128), :], send_sem.at[4])
    wait_bytes(query_all.at[pl.ds(0, 31 * 32), :], send_sem.at[5])
    wait_bytes(key_all.at[pl.ds(0, 3 * 1024), :], send_sem.at[6])
    query_on.wait_send()
    for chunk in range(4):
        wait_bytes(
            value_all.at[pl.ds(0, 7 * PIECE), pl.ds(chunk * 1024, 1024)], value_out_sem.at[chunk]
        )
    stats_out.wait_send()
    for block in range(8):
        part_copy(block).wait_send()
    wait_bytes(att_send.at[pl.ds(0, 31 * 32), :], send_sem.at[10])
    wait_bytes(sum_home.at[pl.ds(0, 127), :], send_sem.at[8])

    home_copy.wait()
    inverse_copy.wait()
    att_copy.wait()

    @pl.when(me < NC - 1)
    def _():
        for which, stream in enumerate(streams):
            wait_bytes(stream.at[pl.ds(TOK - 16, 16), :], halo_send.at[which])


def finish_kernel(
    home_hbm, att_hbm, inverse_hbm, gain_hbm, hyena_out, attn_out,
    home, attended, inverse, out_gain, sem,
):
    loads = [
        pltpu.make_async_copy(src, dst, sem.at[index])
        for index, (src, dst) in enumerate(
            (
                (home_hbm, home),
                (att_hbm, attended),
                (inverse_hbm, inverse),
                (gain_hbm, out_gain),
            )
        )
    ]
    for load in loads:
        load.start()
    for load in loads:
        load.wait()
    column = jnp.broadcast_to(inverse[0:1, :], (TOK, TOK)).T
    for head in range(8):
        cols = slice(head * DH, (head + 1) * DH)
        hyena_out[:, cols] = home[cols, :].astype(F32).T.astype(BF16)
        part = attended[:, cols].astype(F32)
        attn_out[:, cols] = (part * column * out_gain[0:1, cols]).astype(BF16)


def shards(
    queries, key_vectors, stream_gate, stream_key, stream_value,
    short_filter, long_filter, skip_gain, out_gain,
):
    vmem = pl.BlockSpec(memory_space=pltpu.VMEM)
    flat = pltpu.VMEM((NC * PIECE, TOK), BF16)
    dma = pltpu.SemaphoreType.DMA
    constants = dft_constants()
    shape = jax.ShapeDtypeStruct(stream_gate.shape, BF16)
    home, attended, inverse = pl.pallas_call(
        kernel,
        out_shape=(
            jax.ShapeDtypeStruct((NC * PIECE, TOK), BF16),
            shape,
            jax.ShapeDtypeStruct((8, TOK), F32),
        ),
        in_specs=[pl.BlockSpec(memory_space=pltpu.HBM)] * 13,
        out_specs=(pl.BlockSpec(memory_space=pltpu.HBM),) * 3,
        scratch_shapes=[
            *[pltpu.VMEM((TOK, 1024), BF16)] * 3,
            pltpu.VMEM((3, 3, 1024), F32),
            pltpu.VMEM((1024, TOK), F32),
            pltpu.VMEM((8, DH), F32),
            *[pltpu.VMEM(c.shape, c.dtype) for c in constants],
            pltpu.VMEM((3, 16, 1024), BF16),
            flat, flat, flat, flat, flat, flat,
            pltpu.VMEM((PIECE, NC * TOK), BF16),
            flat,
            pltpu.VMEM((NC * PIECE, TOK), F32),
            pltpu.VMEM((NC * PIECE, 2 * TOK), BF16),
            pltpu.VMEM((NC * PIECE, 2 * TOK), F32),
            pltpu.VMEM((NC * PIECE, 2 * TOK), F32),
            pltpu.VMEM((DH, DH), F32),
            pltpu.VMEM((2048, DH), BF16),
            pltpu.VMEM((4096, DH), BF16),
            pltpu.VMEM((DH, 4096), BF16),
            pltpu.VMEM((4096, QB), F32),
            pltpu.VMEM((4096, QB), F32),
            pltpu.VMEM((SPAN, QB), F32),
            pltpu.VMEM((36 * SPAN, QB), BF16),
            pltpu.VMEM((16, QB), F32),
            pltpu.VMEM((16, QB), F32),
            pltpu.VMEM((8, DH, QB), F32),
            pltpu.VMEM((8, DH, 128), F32),
            pltpu.VMEM((8, DH, 128), BF16),
            pltpu.VMEM((8, DH, 128), BF16),
            flat,
            pltpu.VMEM((TOK, 1024), BF16),
            pltpu.VMEM((8, TOK), F32),
            pltpu.VMEM((128, TOK), F32),
            pltpu.VMEM((8, TOK), F32),
            dma((12,)), dma((12,)), dma((3,)), dma((3,)), dma((8,)), dma((8,)),
            dma((17,)), dma((4,)), dma((4,)), pltpu.SemaphoreType.REGULAR,
        ],
        compiler_params=pltpu.CompilerParams(
            collective_id=0, has_side_effects=True, vmem_limit_bytes=63 * 2**20
        ),
    )(
        queries, key_vectors, stream_gate, stream_key, stream_value, short_filter, long_filter,
        skip_gain.reshape(8, DH), *constants,
    )
    return pl.pallas_call(
        finish_kernel,
        out_shape=(shape, shape),
        in_specs=[pl.BlockSpec(memory_space=pltpu.HBM)] * 4,
        out_specs=(vmem, vmem),
        scratch_shapes=[
            flat,
            pltpu.VMEM((TOK, 1024), BF16),
            pltpu.VMEM((8, TOK), F32),
            pltpu.VMEM((1, 1024), F32),
            dma((4,)),
        ],
        compiler_params=pltpu.CompilerParams(vmem_limit_bytes=63 * 2**20),
    )(home, attended, inverse, out_gain.reshape(1, 1024))


def solution(mesh):
    in_specs = (
        P("ctx", "tp"),
        P("ctx", "tp"),
        P("ctx", "tp"),
        P("ctx", "tp"),
        P("ctx", "tp"),
        P(None, None, "tp"),
        P("tp", "ctx"),
        P("tp"),
        P("tp"),
    )
    out_specs = (P("ctx", "tp"), P("ctx", "tp"))
    return jax.shard_map(shards, mesh=mesh, in_specs=in_specs, out_specs=out_specs, check_vma=False)
```

```python
import math

import jax
import jax.numpy as jnp
import numpy as np
from jax import lax
from jax.experimental import pallas as pl
from jax.experimental.pallas import tpu as pltpu
from jax.sharding import PartitionSpec as P

DH = 128
HC = 4096
NC = 64
TOK = 128
PIECE = 16
F32 = jnp.float32
BF16 = jnp.bfloat16
SPAN = 512
QB = 256
LOW = -1e30
SCALE = math.log2(math.e) / math.sqrt(DH)


def block_of(dev):
    return (dev // 2) % 8 * 8 + dev // 16 * 2 + dev % 2


def slot_of(dev):
    return dev % 2 * 32 + dev // 2


def dft_constants():
    slots = np.arange(NC)
    first = (2 * (slots % 32) + slots // 32).astype(np.float64)
    freq = np.arange(NC) + 0.25
    inner = np.arange(TOK)
    outer = 2 * np.pi * freq[:, None] * first[None, :] / NC
    turn = 2 * np.pi * freq[:, None] * inner[None, :] / (NC * TOK)
    mix = 2 * np.pi * (inner[:, None] * inner[None, :] % TOK) / TOK
    cos, sin = np.cos(mix), np.sin(mix)
    outer_in = np.concatenate([np.cos(outer), np.sin(outer)], axis=0)
    outer_out = np.concatenate([np.cos(outer), np.sin(outer)], axis=0).T / (NC * TOK)
    inner_in = np.block([[cos, sin], [-sin, cos]])
    inner_out = np.block([[cos, -sin], [sin, cos]])
    turns = np.stack([np.cos(turn), np.sin(turn)])
    return (
        jnp.asarray(outer_in, BF16),
        jnp.asarray(turns, F32),
        jnp.asarray(inner_in, BF16),
        jnp.asarray(inner_out, BF16),
        jnp.asarray(outer_out, BF16),
    )


def rows16(index):
    return pl.ds(pl.multiple_of(index * PIECE, PIECE), PIECE)


def remote(src, dst, send_sem, recv_sem, dev):
    return pltpu.make_async_remote_copy(
        src_ref=src,
        dst_ref=dst,
        send_sem=send_sem,
        recv_sem=recv_sem,
        device_id={"ctx": dev},
        device_id_type=pl.DeviceIdType.MESH,
    )


def wait_bytes(ref, sem):
    pltpu.make_async_copy(ref, ref, sem).wait()


def mix_taps(stream, halo, taps, which, cols):
    values = stream[:, cols].astype(F32)
    behind = halo[which, :, cols].astype(F32)
    row = lax.broadcasted_iota(jnp.int32, values.shape, 0)
    once = jnp.where(row == 0, behind[15:16], pltpu.roll(values, 1, 0))
    twice = pltpu.roll(values, 2, 0)
    twice = jnp.where(row == 0, behind[14:15], jnp.where(row == 1, behind[15:16], twice))
    mixed = (
        taps[which, 0:1, cols] * values
        + taps[which, 1:2, cols] * once
        + taps[which, 2:3, cols] * twice
    )
    return mixed.astype(BF16)


def spectrum(recv, wide, half, spec, outer_in, turns, inner_in):
    wide[...] = recv[...].astype(F32)
    turn_re, turn_im = turns[0], turns[1]
    for chan in range(0, PIECE, 2):
        pair = [wide[pl.ds(chan + k, NC, stride=PIECE), :].astype(BF16) for k in range(2)]
        both = jnp.dot(outer_in[...], jnp.concatenate(pair, axis=1), preferred_element_type=F32)
        for k in range(2):
            re, im = both[:NC, k * TOK : (k + 1) * TOK], both[NC:, k * TOK : (k + 1) * TOK]
            at = pl.ds((chan + k) * NC, NC)
            half[at, 0:TOK] = (re * turn_re - im * turn_im).astype(BF16)
            half[at, TOK : 2 * TOK] = (re * turn_im + im * turn_re).astype(BF16)
    for part in range(4):
        at = pl.ds(part * 256, 256)
        spec[at, :] = jnp.dot(half[at, :], inner_in[...], preferred_element_type=F32)


def multiply_back(spec_x, spec_h, half, wide, turns, inner_out, outer_out):
    turn_re, turn_im = turns[0], turns[1]
    for part in range(4):
        at = pl.ds(part * 256, 256)
        xr, xi = spec_x[at, 0:TOK], spec_x[at, TOK : 2 * TOK]
        hr, hi = spec_h[at, 0:TOK], spec_h[at, TOK : 2 * TOK]
        half[at, 0:TOK] = (xr * hr - xi * hi).astype(BF16)
        half[at, TOK : 2 * TOK] = (xr * hi + xi * hr).astype(BF16)
    for chan in range(0, PIECE, 2):
        back = jnp.dot(
            half[pl.ds(chan * NC, 2 * NC), :], inner_out[...], preferred_element_type=F32
        )
        pair = []
        for k in range(2):
            re, im = back[k * NC : (k + 1) * NC, :TOK], back[k * NC : (k + 1) * NC, TOK:]
            turned = jnp.concatenate(
                [re * turn_re + im * turn_im, im * turn_re - re * turn_im], axis=0
            )
            pair.append(turned.astype(BF16))
        both = jnp.dot(outer_out[...], jnp.concatenate(pair, axis=1), preferred_element_type=F32)
        for k in range(2):
            wide[pl.ds(chan + k, NC, stride=PIECE), :] = both[:, k * TOK : (k + 1) * TOK]


def span(chunk):
    return pl.ds(pl.multiple_of(chunk * SPAN, SPAN), SPAN)


def visible_bias(core, across):
    row = lax.broadcasted_iota(jnp.int32, (SPAN, QB), 0)
    lane = lax.broadcasted_iota(jnp.int32, (SPAN, QB), 1)
    key_pos = row // 128 * 256 + core * 128 + row % 128
    parity = jnp.where(lane < 128, core, 1 - core)
    query_pos = lane % 128 // 32 * 256 + parity * 128 + across * 32 + lane % 32
    return jnp.where(key_pos <= query_pos, 0.0, LOW)


def attend_scores(core, queries, keys, score_slots, bias, weights, stats):
    def both_halves(block):
        own = queries[pl.ds(pl.multiple_of(core * 1024 + block * 128, 128), 128), :]
        other = queries[pl.ds(pl.multiple_of((1 - core) * 1024 + block * 128, 128), 128), :]
        return jnp.concatenate([own, other], axis=0)

    def score(block, chunk, run_max, masked):
        here = lax.dot_general(
            keys[span(chunk), :],
            both_halves(block),
            (((1,), (1,)), ((), ())),
            preferred_element_type=F32,
        )
        if masked:
            here = here + bias[...]
        score_slots[block % 2][span(chunk), :] = here
        return jnp.maximum(run_max, here.reshape(SPAN // 8, 8, QB).max(axis=0))

    def weigh(block, chunk, top, total):
        terms = jnp.exp2(score_slots[block % 2][span(chunk), :] * SCALE - top)
        weights[span(block * (block + 1) // 2 + chunk), :] = terms.astype(BF16)
        return total + terms.reshape(SPAN // 8, 8, QB).sum(axis=0)

    lowest = jnp.full((8, QB), LOW, F32)
    none = jnp.zeros((8, QB), F32)
    run_max = lax.fori_loop(0, 7, lambda chunk, run: score(7, chunk, run, False), lowest, unroll=7)
    run_max = score(7, 7, run_max, True)
    for block in range(7, -1, -1):
        top = run_max.max(axis=0, keepdims=True) * SCALE

        def beside(chunk, carry, block=block, top=top):
            total, run = carry
            return (weigh(block, chunk, top, total), score(block - 1, chunk, run, False))

        total, run_max = lax.fori_loop(0, block - 1, beside, (none, lowest), unroll=2)
        if block > 0:
            total = weigh(block, block - 1, top, total)
            run_max = score(block - 1, block - 1, run_max, True)
        total = weigh(block, block, top, total)
        stats[block : block + 1, :] = top
        stats[8 + block : 9 + block, :] = total.sum(axis=0, keepdims=True)


def value_chunk(chunk, values, weights, totals):
    lanes = slice(chunk * 1024, (chunk + 1) * 1024)
    for block in range(2 * chunk, 8):
        first = (block * (block + 1) // 2 + 2 * chunk) * SPAN
        reach = SPAN if block == 2 * chunk else 2 * SPAN
        add = jnp.dot(
            values[:, lanes][:, :reach],
            weights[first : first + reach, :],
            preferred_element_type=F32,
        )
        totals[block] = add if chunk == 0 else totals[block] + add


def share_factor(block, stats, other_stats):
    top, count = stats[pl.ds(block, 1), :], stats[pl.ds(8 + block, 1), :]
    swap = lambda v: jnp.concatenate([v[:, 128:], v[:, :128]], axis=1)
    other_top = swap(other_stats[pl.ds(block, 1), :])
    other_count = swap(other_stats[pl.ds(8 + block, 1), :])
    both_top = jnp.maximum(top, other_top)
    mine = jnp.exp2(top - both_top)
    whole = mine * count + jnp.exp2(other_top - both_top) * other_count
    return mine / whole


def kernel(
    queries, key_vectors, gate_hbm, key_hbm, value_hbm,
    taps_hbm, filter_hbm, skip_hbm,
    outer_in_hbm, turns_hbm, inner_in_hbm, inner_out_hbm, outer_out_hbm,
    home_out, att_out, inverse_out,
    stream_gate, stream_key, stream_value, taps, long_filter, skip_gain,
    outer_in, turns, inner_in, inner_out, outer_out,
    halo, filt_send, prod_send, gate_send, filt_recv, prod_recv, gate_recv,
    hyena, home, wide, half, spec_x, spec_h, column,
    query_all, key_all, value_all, scores_even, scores_odd, bias, weights, stats, other_stats,
    totals, own_part, part_send, part_recv, att_send, att_home, sum_own, sum_home, inverse,
    send_sem, recv_sem, halo_send, halo_recv, part_out, part_in,
    load_sem, value_out_sem, value_in_sem, plane_ready,
):
    me = lax.axis_index("ctx")
    tp = lax.axis_index("tp")
    across, depth, core = me // 16, (me // 2) % 8, me % 2
    pair, sibling = me // 2, me + 1 - 2 * core
    member = across * 2 + core
    my_block, my_slot = block_of(me), slot_of(me)
    barrier = pltpu.get_barrier_semaphore()

    def greet(step, unused):
        pl.semaphore_signal(
            barrier,
            inc=1,
            device_id={"ctx": lax.rem(me + step, NC)},
            device_id_type=pl.DeviceIdType.MESH,
        )
        return unused

    lax.fori_loop(1, NC, greet, 0)
    for step in range(1, 4):
        pl.semaphore_signal(
            barrier,
            inc=1,
            device_id={"tp": lax.rem(tp + step, 4)},
            device_id_type=pl.DeviceIdType.MESH,
        )
    loads = [
        pltpu.make_async_copy(src, dst, load_sem.at[index])
        for index, (src, dst) in enumerate(
            (
                (filter_hbm, long_filter),
                (taps_hbm, taps),
                (key_hbm, stream_key),
                (value_hbm, stream_value),
                (gate_hbm, stream_gate),
                (outer_in_hbm, outer_in),
                (turns_hbm, turns),
                (inner_in_hbm, inner_in),
                (inner_out_hbm, inner_out),
                (outer_out_hbm, outer_out),
                (skip_hbm, skip_gain),
            )
        )
    ]
    key_rows = pl.ds(pl.multiple_of(pair * 128, 128), 128)
    query_rows = pl.ds(pl.multiple_of(core * 1024 + pair * 32, 32), 32)
    across_rows = pl.ds(pl.multiple_of(across * 32, 32), 32)
    my_cols = pl.ds(pl.multiple_of(depth * DH, DH), DH)
    loads.append(
        pltpu.make_async_copy(key_vectors.at[:, my_cols], key_all.at[key_rows, :], load_sem.at[12])
    )
    loads.append(
        pltpu.make_async_copy(
            queries.at[across_rows, my_cols], query_all.at[query_rows, :], load_sem.at[13]
        )
    )
    for load in loads:
        load.start()

    @pl.when(me == 0)
    def _():
        halo[...] = jnp.zeros_like(halo)

    loads[0].wait()
    filt_send[...] = long_filter[...].astype(BF16)
    pl.semaphore_wait(barrier, NC - 1 + 3)
    for step in range(1, 4):
        pl.semaphore_signal(
            plane_ready,
            inc=1,
            device_id={"tp": lax.rem(tp + step, 4)},
            device_id_type=pl.DeviceIdType.MESH,
        )

    streams = (gate_hbm, key_hbm, value_hbm)

    @pl.when(me < NC - 1)
    def _():
        for which, stream in enumerate(streams):
            remote(
                stream.at[pl.ds(TOK - 16, 16), :],
                halo.at[which],
                halo_send.at[which],
                halo_recv.at[which],
                me + 1,
            ).start()

    def key_out(step, unused):
        head = lax.rem(depth + step, 8)
        remote(
            key_vectors.at[:, pl.ds(pl.multiple_of(head * DH, DH), DH)],
            key_all.at[key_rows, :],
            send_sem.at[4],
            recv_sem.at[4],
            across * 16 + head * 2 + core,
        ).start()
        return unused

    lax.fori_loop(1, 8, key_out, 0)

    def scatter(send, recv, index):
        def one(step, unused):
            dev = lax.rem(me + step, NC)
            remote(
                send.at[rows16(block_of(dev)), :],
                recv.at[rows16(my_slot), :],
                send_sem.at[index],
                recv_sem.at[index],
                dev,
            ).start()
            return unused

        lax.fori_loop(1, NC, one, 0)
        recv[rows16(my_slot), :] = send[rows16(my_block), :]

    rest = pl.ds(0, (NC - 1) * PIECE)
    scatter(filt_send, filt_recv, 0)

    for load in loads[1:5]:
        load.wait()

    @pl.when(me > 0)
    def _():
        for which in range(3):
            wait_bytes(halo.at[which], halo_recv.at[which])

    def columns(head, unused):
        cols = pl.ds(pl.multiple_of(head * DH, DH), DH)
        key_feat = mix_taps(stream_key, halo, taps, 1, cols)
        value_feat = mix_taps(stream_value, halo, taps, 2, cols)
        product = key_feat.astype(F32) * value_feat.astype(F32)
        prod_send[cols, :] = product.T.astype(BF16)
        return unused

    lax.fori_loop(0, 8, columns, 0, unroll=2)
    scatter(prod_send, prod_recv, 1)

    def gate_columns(head, unused):
        cols = pl.ds(pl.multiple_of(head * DH, DH), DH)
        gate_feat = mix_taps(stream_gate, halo, taps, 0, cols)
        gate_send[cols, :] = gate_feat.astype(F32).T.astype(BF16)
        return unused

    lax.fori_loop(0, 8, gate_columns, 0, unroll=2)
    scatter(gate_send, gate_recv, 2)

    def query_out(step, unused):
        goal = lax.rem(pair + step, 32)
        remote(
            queries.at[
                pl.ds(pl.multiple_of(goal // 8 * 32, 32), 32),
                pl.ds(pl.multiple_of(goal % 8 * DH, DH), DH),
            ],
            query_all.at[query_rows, :],
            send_sem.at[5],
            recv_sem.at[5],
            goal * 2 + core,
        ).start()
        return unused

    lax.fori_loop(1, 32, query_out, 0)

    for load in loads[5:]:
        load.wait()
    wait_bytes(key_all.at[pl.ds(0, 7 * 128), :], recv_sem.at[4])
    keys_here = pl.ds(pl.multiple_of(across * 1024, 1024), 1024)

    def key_on(step, unused):
        remote(
            key_all.at[keys_here, :],
            key_all.at[keys_here, :],
            send_sem.at[6],
            recv_sem.at[6],
            lax.rem(across + step, 4) * 16 + depth * 2 + core,
        ).start()
        return unused

    lax.fori_loop(1, 4, key_on, 0)

    head_row = skip_gain[pl.ds(depth, 1), :]
    column[...] = jnp.broadcast_to(head_row, (DH, DH)).T
    skip_tile = column[rows16(my_block % 8), :]
    bias[...] = visible_bias(core, across)

    wait_bytes(filt_recv.at[rest, :], recv_sem.at[0])
    spectrum(filt_recv, wide, half, spec_h, outer_in, turns, inner_in)
    wait_bytes(prod_recv.at[rest, :], recv_sem.at[1])

    spectrum(prod_recv, wide, half, spec_x, outer_in, turns, inner_in)
    multiply_back(spec_x, spec_h, half, wide, turns, inner_out, outer_out)
    wait_bytes(gate_recv.at[rest, :], recv_sem.at[2])

    def gated(slot, unused):
        at = rows16(slot)
        inner = wide[at, :] + skip_tile * prod_recv[at, :].astype(F32)
        lanes = pl.ds(pl.multiple_of(slot * TOK, TOK), TOK)
        hyena[:, lanes] = (gate_recv[at, :].astype(F32) * inner).astype(BF16)
        return unused

    for chunk in range(4):
        lax.fori_loop(chunk * 8, chunk * 8 + 8, gated, 0, unroll=True)
        lax.fori_loop(32 + chunk * 8, 32 + chunk * 8 + 8, gated, 0, unroll=True)

        def value_out(step, unused):
            goal = lax.rem(member + step, 8)
            lanes = pl.ds(pl.multiple_of(goal % 2 * 4096 + chunk * 1024, 1024), 1024)
            remote(
                hyena.at[:, lanes],
                value_all.at[rows16(member), pl.ds(chunk * 1024, 1024)],
                value_out_sem.at[chunk],
                value_in_sem.at[chunk],
                goal // 2 * 16 + depth * 2 + goal % 2,
            ).start()
            return unused

        lax.fori_loop(1, 8, value_out, 0)
        lanes = pl.ds(pl.multiple_of(core * 4096 + chunk * 1024, 1024), 1024)
        value_all[rows16(member), pl.ds(chunk * 1024, 1024)] = hyena[:, lanes]

    def go_home(step, unused):
        dev = lax.rem(me + step, NC)
        remote(
            hyena.at[:, pl.ds(pl.multiple_of(slot_of(dev) * TOK, TOK), TOK)],
            home.at[rows16(my_block), :],
            send_sem.at[3],
            recv_sem.at[3],
            dev,
        ).start()
        return unused

    lax.fori_loop(1, NC, go_home, 0, unroll=9)
    home[rows16(my_block), :] = hyena[:, pl.ds(pl.multiple_of(my_slot * TOK, TOK), TOK)]

    wait_bytes(query_all.at[pl.ds(0, 31 * 32), :], recv_sem.at[5])
    queries_here = pl.ds(pl.multiple_of(core * 1024, 1024), 1024)
    query_on = remote(
        query_all.at[queries_here, :],
        query_all.at[queries_here, :],
        send_sem.at[7],
        recv_sem.at[7],
        sibling,
    )
    query_on.start()
    wait_bytes(key_all.at[pl.ds(0, 3 * 1024), :], recv_sem.at[6])
    query_on.wait_recv()

    attend_scores(core, query_all, key_all, (scores_even, scores_odd), bias, weights, stats)
    stats_out = remote(stats, other_stats, send_sem.at[9], recv_sem.at[9], sibling)
    stats_out.start()

    stats_out.wait_recv()
    pl.semaphore_wait(plane_ready, 3)

    def part_copy(block):
        return remote(
            part_send.at[block],
            part_recv.at[block],
            part_out.at[block],
            part_in.at[block],
            sibling,
        )

    def share(block):
        total = totals[block] * share_factor(block, stats, other_stats)
        own_part[block] = total[:, :128]
        part_send[block] = total[:, 128:].astype(BF16)
        part_copy(block).start()

    def sum_copy(block, goal, row):
        return pltpu.make_async_remote_copy(
            src_ref=sum_own.at[pl.ds(block, 1), :],
            dst_ref=sum_home.at[pl.ds(tp * 32 + pair, 1), :],
            send_sem=send_sem.at[8],
            recv_sem=recv_sem.at[8],
            device_id={"ctx": goal * 2 + core, "tp": row},
            device_id_type=pl.DeviceIdType.MESH,
        )

    def settle(block):
        part_copy(block).wait_recv()
        whole = (own_part[block] + part_recv[block].astype(F32)).astype(BF16).astype(F32)
        att_send[pl.ds(block * 128, 128), :] = whole.T.astype(BF16)
        sum_own[block : block + 1, :] = (whole * whole).sum(axis=0, keepdims=True)

        def send(step, unused):
            goal = block * 4 + lax.rem(depth + step, 4)
            rows = pl.ds(pl.multiple_of(goal * 32, 32), 32)

            @pl.when(goal != pair)
            def _():
                remote(
                    att_send.at[rows, :],
                    att_home.at[across_rows, my_cols],
                    send_sem.at[10],
                    recv_sem.at[10],
                    goal * 2 + core,
                ).start()
                sum_copy(block, goal, tp).start()

            @pl.when(goal == pair)
            def _():
                att_home[across_rows, my_cols] = att_send[rows, :]
                sum_home[pl.ds(tp * 32 + pair, 1), :] = sum_own[pl.ds(block, 1), :]

            for other in range(1, 4):
                sum_copy(block, goal, lax.rem(tp + other, 4)).start()
            return unused

        lax.fori_loop(0, 4, send, 0, unroll=True)

    for chunk in range(4):
        wait_bytes(
            value_all.at[pl.ds(0, 7 * PIECE), pl.ds(chunk * 1024, 1024)], value_in_sem.at[chunk]
        )
        value_chunk(chunk, value_all, weights, totals)
        share(2 * chunk)
        share(2 * chunk + 1)
        settle(2 * chunk)
        settle(2 * chunk + 1)

    wait_bytes(home.at[rest, :], recv_sem.at[3])

    home_copy = pltpu.make_async_copy(home, home_out, load_sem.at[14])
    home_copy.start()

    wait_bytes(sum_home.at[pl.ds(0, 127), :], recv_sem.at[8])
    lane = lax.broadcasted_iota(jnp.int32, (1, TOK), 1)
    mean = jnp.zeros((1, TOK), F32)
    for group in range(4):
        part = sum_home[8 * group : 8 * group + 8, :]
        for row in range(1, 4):
            part = part + sum_home[32 * row + 8 * group : 32 * row + 8 * group + 8, :]
        part = jnp.broadcast_to(part.sum(axis=0, keepdims=True), (8, TOK))
        part = pltpu.roll(part, (group + 4 - pair % 4) * 32 % TOK, 1)
        mean = jnp.where(lane // 32 == group, part[0:1, :], mean)
    mean = mean * (1.0 / HC)
    inverse[...] = jnp.broadcast_to(lax.rsqrt(mean + 1e-05), (8, TOK))
    inverse_copy = pltpu.make_async_copy(inverse, inverse_out, load_sem.at[15])
    inverse_copy.start()
    wait_bytes(att_send.at[pl.ds(0, 31 * 32), :], recv_sem.at[10])
    att_copy = pltpu.make_async_copy(att_home, att_out, load_sem.at[16])
    att_copy.start()

    for index, send in enumerate((filt_send, prod_send, gate_send, home)):
        wait_bytes(send.at[rest, :], send_sem.at[index])
    wait_bytes(key_all.at[pl.ds(0, 7 * 128), :], send_sem.at[4])
    wait_bytes(query_all.at[pl.ds(0, 31 * 32), :], send_sem.at[5])
    wait_bytes(key_all.at[pl.ds(0, 3 * 1024), :], send_sem.at[6])
    query_on.wait_send()
    for chunk in range(4):
        wait_bytes(
            value_all.at[pl.ds(0, 7 * PIECE), pl.ds(chunk * 1024, 1024)], value_out_sem.at[chunk]
        )
    stats_out.wait_send()
    for block in range(8):
        part_copy(block).wait_send()
    wait_bytes(att_send.at[pl.ds(0, 31 * 32), :], send_sem.at[10])
    wait_bytes(sum_home.at[pl.ds(0, 127), :], send_sem.at[8])

    home_copy.wait()
    inverse_copy.wait()
    att_copy.wait()

    @pl.when(me < NC - 1)
    def _():
        for which, stream in enumerate(streams):
            wait_bytes(stream.at[pl.ds(TOK - 16, 16), :], halo_send.at[which])


def finish_kernel(
    home_hbm, att_hbm, inverse_hbm, gain_hbm, hyena_out, attn_out,
    home, attended, inverse, out_gain, hyena_here, attn_here, sem,
):
    loads = [
        pltpu.make_async_copy(src, dst, sem.at[index])
        for index, (src, dst) in enumerate(
            (
                (home_hbm, home),
                (att_hbm, attended),
                (inverse_hbm, inverse),
                (gain_hbm, out_gain),
            )
        )
    ]
    for load in loads:
        load.start()
    loads[0].wait()
    for head in range(8):
        cols = slice(head * DH, (head + 1) * DH)
        hyena_here[:, cols] = home[cols, :].astype(F32).T.astype(BF16)
    hyena_write = pltpu.make_async_copy(hyena_here, hyena_out, sem.at[4])
    hyena_write.start()
    for load in loads[1:]:
        load.wait()
    column = jnp.broadcast_to(inverse[0:1, :], (TOK, TOK)).T
    for head in range(8):
        cols = slice(head * DH, (head + 1) * DH)
        part = attended[:, cols].astype(F32)
        attn_here[:, cols] = (part * column * out_gain[0:1, cols]).astype(BF16)
    attn_write = pltpu.make_async_copy(attn_here, attn_out, sem.at[5])
    attn_write.start()
    hyena_write.wait()
    attn_write.wait()


def shards(
    queries, key_vectors, stream_gate, stream_key, stream_value,
    short_filter, long_filter, skip_gain, out_gain,
):
    vmem = pl.BlockSpec(memory_space=pltpu.VMEM)
    flat = pltpu.VMEM((NC * PIECE, TOK), BF16)
    dma = pltpu.SemaphoreType.DMA
    constants = dft_constants()
    shape = jax.ShapeDtypeStruct(stream_gate.shape, BF16)
    home, attended, inverse = pl.pallas_call(
        kernel,
        out_shape=(
            jax.ShapeDtypeStruct((NC * PIECE, TOK), BF16),
            shape,
            jax.ShapeDtypeStruct((8, TOK), F32),
        ),
        in_specs=[pl.BlockSpec(memory_space=pltpu.HBM)] * 13,
        out_specs=(pl.BlockSpec(memory_space=pltpu.HBM),) * 3,
        scratch_shapes=[
            *[pltpu.VMEM((TOK, 1024), BF16)] * 3,
            pltpu.VMEM((3, 3, 1024), F32),
            pltpu.VMEM((1024, TOK), F32),
            pltpu.VMEM((8, DH), F32),
            *[pltpu.VMEM(c.shape, c.dtype) for c in constants],
            pltpu.VMEM((3, 16, 1024), BF16),
            flat, flat, flat, flat, flat, flat,
            pltpu.VMEM((PIECE, NC * TOK), BF16),
            flat,
            pltpu.VMEM((NC * PIECE, TOK), F32),
            pltpu.VMEM((NC * PIECE, 2 * TOK), BF16),
            pltpu.VMEM((NC * PIECE, 2 * TOK), F32),
            pltpu.VMEM((NC * PIECE, 2 * TOK), F32),
            pltpu.VMEM((DH, DH), F32),
            pltpu.VMEM((2048, DH), BF16),
            pltpu.VMEM((4096, DH), BF16),
            pltpu.VMEM((DH, 4096), BF16),
            pltpu.VMEM((4096, QB), F32),
            pltpu.VMEM((4096, QB), F32),
            pltpu.VMEM((SPAN, QB), F32),
            pltpu.VMEM((36 * SPAN, QB), BF16),
            pltpu.VMEM((16, QB), F32),
            pltpu.VMEM((16, QB), F32),
            pltpu.VMEM((8, DH, QB), F32),
            pltpu.VMEM((8, DH, 128), F32),
            pltpu.VMEM((8, DH, 128), BF16),
            pltpu.VMEM((8, DH, 128), BF16),
            flat,
            pltpu.VMEM((TOK, 1024), BF16),
            pltpu.VMEM((8, TOK), F32),
            pltpu.VMEM((128, TOK), F32),
            pltpu.VMEM((8, TOK), F32),
            dma((12,)), dma((12,)), dma((3,)), dma((3,)), dma((8,)), dma((8,)),
            dma((17,)), dma((4,)), dma((4,)), pltpu.SemaphoreType.REGULAR,
        ],
        compiler_params=pltpu.CompilerParams(
            collective_id=0, has_side_effects=True, vmem_limit_bytes=63 * 2**20
        ),
    )(
        queries, key_vectors, stream_gate, stream_key, stream_value, short_filter, long_filter,
        skip_gain.reshape(8, DH), *constants,
    )
    return pl.pallas_call(
        finish_kernel,
        out_shape=(shape, shape),
        in_specs=[pl.BlockSpec(memory_space=pltpu.HBM)] * 4,
        out_specs=(pl.BlockSpec(memory_space=pltpu.HBM),) * 2,
        scratch_shapes=[
            flat,
            pltpu.VMEM((TOK, 1024), BF16),
            pltpu.VMEM((8, TOK), F32),
            pltpu.VMEM((1, 1024), F32),
            pltpu.VMEM((TOK, 1024), BF16),
            pltpu.VMEM((TOK, 1024), BF16),
            dma((6,)),
        ],
        compiler_params=pltpu.CompilerParams(vmem_limit_bytes=63 * 2**20),
    )(home, attended, inverse, out_gain.reshape(1, 1024))


def solution(mesh):
    in_specs = (
        P("ctx", "tp"),
        P("ctx", "tp"),
        P("ctx", "tp"),
        P("ctx", "tp"),
        P("ctx", "tp"),
        P(None, None, "tp"),
        P("tp", "ctx"),
        P("tp"),
        P("tp"),
    )
    out_specs = (P("ctx", "tp"), P("ctx", "tp"))
    return jax.shard_map(shards, mesh=mesh, in_specs=in_specs, out_specs=out_specs, check_vma=False)
```
